32 devices in a mesh: ev: 4 (over z), blk: 8 (over y, x, core).
Axes of the slice: x: 2, y: 2, z: 4, core: 2. Of those that a mesh axis runs over, the one named last changes fastest.
Arguments:
- kernel_tiles: bfloat16 [4, 8, 6, 6, 2048], P('ev', 'blk'), may hold values from -6 to 6
- region: int32 [4, 8, 6], P('ev', 'blk'), may hold values from 0 to 15, as said below
- band_width: int32 [8], replicated, may hold values from 2 to 16
Outputs:
- smoothed: float32 [3, 16, 32768], P(None, None, ('ev', 'blk'))
The draws below stay inside these ranges and needn't reach their ends.
Inputs may be any that keep to these rules, and one draw needn't show every extreme that they name: `region`: each device's 6 entries are distinct, and no more than 2 of them lie in one lateral section (numbers s * 4 to s * 4 + 3); every device has 2 in some section.
All inputs are finite; a program needn't handle non-finite values.
Results may differ from the reference program's by a relative error of at most 0.015.
Values may be sent and summed in bfloat16 or wider, within the bound.
A program may use at most 64 MiB of HBM per device.

```python
import jax
import jax.numpy as jnp
from jax import lax

NT = 4
CAP = 2
LAYERS = 8
ZS = 2
TW = 2048
EVG = 4
BLKS = 8
KB = 6
Z = 16
LAT = 32768


def draw_region(key, part):
    key = jax.random.fold_in(key, 11)
    key_zero, key_rank, key_tile, key_order = jax.random.split(key, 4)
    count = EVG * BLKS
    zeros_n = jax.random.randint(key_zero, (count, 1), 0, EVG // 4 + 1)
    twos_n = EVG // 2 + zeros_n
    ranks = jax.vmap(lambda k: jax.random.permutation(k, EVG))(jax.random.split(key_rank, count))
    counts = jnp.where(ranks < zeros_n, 0, jnp.where(ranks < zeros_n + twos_n, 2, 1))
    tile_keys = jax.random.split(key_tile, count * EVG)
    within = jax.vmap(lambda k: jax.random.permutation(k, NT))(tile_keys).reshape(count, EVG, NT)[:, :, :CAP]
    section = jnp.arange(EVG, dtype=jnp.int32)[None, :, None]
    ids_all = (section * NT + within).reshape(count, EVG * CAP)
    valid = (jnp.arange(CAP, dtype=jnp.int32)[None, None, :] < counts[:, :, None]).reshape(count, EVG * CAP)
    position = jnp.cumsum(valid.astype(jnp.int32), axis=1) - 1
    slots = jnp.arange(KB, dtype=jnp.int32)
    hit = valid[:, :, None] & (position[:, :, None] == slots[None, None, :])
    packed = jnp.sum(jnp.where(hit, ids_all[:, :, None], 0), axis=1)
    order = jax.vmap(lambda k: jax.random.permutation(k, KB))(jax.random.split(key_order, count))
    mixed = jnp.take_along_axis(packed, order, axis=1)
    return mixed.reshape(EVG, BLKS, KB).astype(jnp.int32)


def plant(result, key, low, largest):
    longest = result.shape.index(max(result.shape))
    spots = []
    for shift in (0, 1):
        where = [jax.random.randint(jax.random.fold_in(key, axis), (), 0, length) for axis, length in enumerate(result.shape)]
        where[longest] = (where[longest] + shift) % result.shape[longest]
        spots.append(tuple(where))
    return result.at[spots[0]].set(low).at[spots[1]].set(largest)


def block_scale(own_key, shape, cuts, smallest, largest):
    loudness, own = 1.0, jax.random.fold_in(own_key, 6)
    for dim, shards_of in cuts:
        heights = jnp.exp(jax.random.uniform(jax.random.fold_in(own, dim), (shards_of,), jnp.float32, smallest / len(cuts), largest / len(cuts)))
        loudness = loudness * jnp.repeat(heights, shape[dim] // shards_of).reshape([-1 if axis == dim else 1 for axis in range(len(shape))])
    return loudness


def normal_values(rng, shape, scale, most, cuts=(), kind=jnp.bfloat16):
    drawn = jax.random.normal(rng, shape, jnp.float32) * scale
    if len(cuts) > 0:
        drawn = block_scale(rng, shape, cuts, -0.22, 0.18) * drawn
    return jnp.clip(drawn, min=-most, max=most).astype(kind)


def setup_inputs(seed: int = 0) -> dict:
    arg_keys = jax.random.split(jax.random.key(seed), 4)
    return {
        "kernel_tiles": normal_values(arg_keys[0], (EVG, BLKS, KB, 3 * ZS, TW), 1.0, 6.0, ((0, 4), (1, 8))),
        "region": draw_region(jax.random.fold_in(arg_keys[3], 71), 0),
        "band_width": plant(jax.random.randint(arg_keys[2], (LAYERS,), 2, 17), jax.random.fold_in(arg_keys[2], 1), 2, 16).astype(jnp.int32),
    }


def build_smoother(band_width, depth):
    rows = jnp.arange(depth, dtype=jnp.int32)
    layer = rows // (depth // LAYERS)
    pick = (layer[:, None] == jnp.arange(LAYERS, dtype=jnp.int32)[None, :]).astype(jnp.int32)
    half = jnp.sum(pick * band_width[None, :], axis=1)
    dist = jnp.abs(rows[:, None] - rows[None, :])
    weight = jnp.maximum(half[:, None] + 1 - dist, 0).astype(jnp.float32)
    return (weight / jnp.sum(weight, axis=1, keepdims=True)).astype(jnp.bfloat16)


def reference(kernel_tiles, region, band_width):
    total = EVG * NT
    targets = jnp.arange(total, dtype=jnp.int32)

    def per_slab(b):
        tiles_b = kernel_tiles[:, b].reshape(EVG, KB, 3 * ZS * TW).astype(jnp.float32)
        ids_b = region[:, b]
        onehot = (ids_b[:, :, None] == targets[None, None, :]).astype(jnp.float32)
        summed = jnp.einsum("ekt,ekx->tx", onehot, tiles_b, precision=lax.Precision.HIGHEST)
        slab = summed.reshape(EVG, NT, 3, ZS, TW).transpose(2, 3, 0, 1, 4).reshape(3, ZS, LAT)
        return slab.astype(jnp.bfloat16)

    slabs = lax.map(per_slab, jnp.arange(BLKS, dtype=jnp.int32))
    gradient = slabs.transpose(1, 0, 2, 3).reshape(3, Z, LAT)
    smoother = build_smoother(band_width, Z)
    return jnp.einsum("ij,cjl->cil", smoother.astype(jnp.float32), gradient.astype(jnp.float32), precision=lax.Precision.HIGHEST)
```

```python
import functools

import jax
import jax.numpy as jnp
from jax import lax
from jax.experimental import pallas as pl
from jax.experimental.pallas import tpu as pltpu
from jax.sharding import PartitionSpec as P

NT = 4
CAP = 2
LAYERS = 8
LANES = 128
TAG = 16
MESH = pl.DeviceIdType.MESH


def log2(n):
    assert n & (n - 1) == 0
    return n.bit_length() - 1


def spread_smoother(band, depth, slabs, cols, block):
    shape = (cols * depth, slabs * block)
    row = lax.broadcasted_iota(jnp.int32, shape, 0)
    col = lax.broadcasted_iota(jnp.int32, shape, 1)
    level = row & (depth - 1)
    within = col & (block - 1)
    levels = depth // slabs
    source = (col >> log2(block)) * levels + (within >> log2(cols))
    layer = level >> log2(depth // LAYERS)
    half = jnp.zeros(shape, jnp.int32)
    for n in range(LAYERS):
        half = jnp.where(layer == n, band[n], half)
    weight = jnp.maximum(half + 1 - jnp.abs(level - source), 0)
    weight = jnp.where(within < levels * cols, weight, 0).astype(jnp.float32)
    total = jnp.sum(weight, axis=1, keepdims=True) * (1.0 / cols)
    same = (row >> log2(depth)) == (within & (cols - 1))
    return jnp.where(same, weight / total, 0.0).astype(jnp.bfloat16)


def kernel(dims, tiles_hbm, region_hbm, band_hbm, out_ref, tiles, region, band, spread, pack, land, stage, grad,
           weights, in_sem, send1, recv1, send2, recv2):
    groups, slabs, count, levels, parts, cols, block = dims
    depth = levels * slabs
    per_tile = slabs // NT
    rows = levels * parts
    me, mine = lax.axis_index("ev"), lax.axis_index("blk")
    peers = [lax.rem(me + j, groups) for j in range(groups)]
    mates = [lax.rem(mine + j, slabs) for j in range(slabs)]

    barrier = pltpu.get_barrier_semaphore()
    for j in range(1, groups):
        pl.semaphore_signal(barrier, inc=1, device_id=(peers[j], mine), device_id_type=MESH)
    for j in range(1, slabs):
        pl.semaphore_signal(barrier, inc=1, device_id=(me, mates[j]), device_id_type=MESH)
    loads = [
        pltpu.make_async_copy(region_hbm, region, in_sem.at[0]),
        pltpu.make_async_copy(tiles_hbm, tiles, in_sem.at[1]),
        pltpu.make_async_copy(band_hbm, band, in_sem.at[2]),
    ]
    for load in loads:
        load.start()
    loads[0].wait()
    ids = [region[k] for k in range(count)]
    loads[1].wait()

    def pack_section(j):
        first, last = jnp.int32(-1), jnp.int32(-1)
        for k in range(count):
            here = (ids[k] >> log2(NT)) == peers[j]
            last = jnp.where(here, k, last)
            first = jnp.where(here & (first < 0), k, first)
        for slot, (entry, there) in enumerate(((first, first >= 0), (last, last != first))):
            entry = jnp.maximum(entry, 0)
            tile = jnp.where(there, region[entry] & (NT - 1), -1)
            pack[0, j, slot * 8 : slot * 8 + 8, :] = jnp.full((8, LANES), tile, jnp.int32).astype(jnp.bfloat16)
            values = tiles[entry].astype(jnp.float32)
            for k in range(parts):
                spread[j, slot, :, k, :] = values[:, k * LANES : (k + 1) * LANES]
            for c in range(3):
                piece = spread[j, slot, c * levels : (c + 1) * levels].reshape(rows, LANES)
                at = TAG + slot * rows
                pack[c, j, at : at + rows, :] = piece.astype(jnp.bfloat16)

    def send_section(c, j):
        at = pl.ds(0, TAG + CAP * rows) if c == 0 else pl.ds(TAG, CAP * rows)
        copy = pltpu.make_async_remote_copy(
            src_ref=pack.at[c, j, at],
            dst_ref=land.at[c, j, at],
            send_sem=send1.at[c, j],
            recv_sem=recv1.at[c, j],
            device_id=(peers[j], mine),
            device_id_type=MESH,
        )
        copy.start()
        return copy

    def send_columns(c, j):
        copy = pltpu.make_async_remote_copy(
            src_ref=stage.at[c, mates[j]],
            dst_ref=grad.at[c, mine],
            send_sem=send2.at[c, j],
            recv_sem=recv2.at[c, j],
            device_id=(me, mates[j]),
            device_id_type=MESH,
        )
        copy.start()
        return copy

    order = list(range(groups - 1, 0, -1))
    sections, columns = {}, {}
    for n, j in enumerate(order):
        pack_section(j)
        if n == 0:
            pl.semaphore_wait(barrier, groups + slabs - 2)
        sections[0, j] = send_section(0, j)
    for c in range(1, 3):
        for j in order:
            sections[c, j] = send_section(c, j)
    pack_section(0)
    loads[2].wait()
    weights[...] = spread_smoother(band, depth, slabs, cols, block)

    for c in range(3):
        sums = [jnp.zeros((levels * parts // 8, 8, LANES), jnp.float32) for _ in range(NT)]
        for j in range(groups):
            if j > 0:
                sections[c, j].wait_recv()
            held = pack if j == 0 else land
            tags = held[0, j, :TAG, :].astype(jnp.float32)
            for slot in range(CAP):
                at = TAG + slot * rows
                term = held[c, j, at : at + rows, :].astype(jnp.float32).reshape(rows // 8, 8, LANES)
                tag = tags[slot * 8 : slot * 8 + 8]
                for t in range(NT):
                    sums[t] += jnp.where((tag == t)[None], term, 0.0)
        for t in range(NT):
            total = sums[t].reshape(levels, parts, LANES)
            for q in range(per_tile):
                piece = total[:, q * cols : (q + 1) * cols, :].reshape(levels * cols, LANES)
                if block > levels * cols:
                    fill = jnp.zeros((block - levels * cols, LANES), jnp.float32)
                    piece = jnp.concatenate([piece, fill], axis=0)
                stage[c, t * per_tile + q] = piece.astype(jnp.bfloat16)
        for j in range(1, slabs):
            columns[c, j] = send_columns(c, j)
        grad[c, mine] = stage[c, mine]

    for c in range(3):
        for j in range(1, slabs):
            columns[c, j].wait_recv()
        gathered = grad[c].reshape(slabs * block, LANES)
        smooth = jnp.dot(weights[...], gathered, preferred_element_type=jnp.float32)
        for k in range(cols):
            out_ref[c, :, k * LANES : (k + 1) * LANES] = smooth[k * depth : (k + 1) * depth]
    for copy in list(sections.values()) + list(columns.values()):
        copy.wait_send()


def shards(kernel_tiles, region, band_width):
    tiles, ids = kernel_tiles[0, 0], region[0, 0]
    groups, slabs = lax.axis_size("ev"), lax.axis_size("blk")
    count, held, width = tiles.shape
    levels = held // 3
    depth = levels * slabs
    parts = width // LANES
    cols = NT * parts // slabs
    block = -(-levels * cols // 16) * 16
    dims = (groups, slabs, count, levels, parts, cols, block)
    rows = levels * parts
    message = TAG + CAP * rows
    return pl.pallas_call(
        functools.partial(kernel, dims),
        out_shape=jax.ShapeDtypeStruct((3, depth, cols * LANES), jnp.float32),
        in_specs=[pl.BlockSpec(memory_space=pl.ANY)] * 3,
        out_specs=pl.BlockSpec(memory_space=pltpu.VMEM),
        scratch_shapes=[
            pltpu.VMEM(tiles.shape, jnp.bfloat16),
            pltpu.SMEM(ids.shape, jnp.int32),
            pltpu.SMEM(band_width.shape, jnp.int32),
            pltpu.VMEM((groups, CAP, held, parts, LANES), jnp.float32),
            pltpu.VMEM((3, groups, message, LANES), jnp.bfloat16),
            pltpu.VMEM((3, groups, message, LANES), jnp.bfloat16),
            pltpu.VMEM((3, slabs, block, LANES), jnp.bfloat16),
            pltpu.VMEM((3, slabs, block, LANES), jnp.bfloat16),
            pltpu.VMEM((cols * depth, slabs * block), jnp.bfloat16),
            pltpu.SemaphoreType.DMA((3,)),
            pltpu.SemaphoreType.DMA((3, groups)),
            pltpu.SemaphoreType.DMA((3, groups)),
            pltpu.SemaphoreType.DMA((3, slabs)),
            pltpu.SemaphoreType.DMA((3, slabs)),
        ],
        compiler_params=pltpu.CompilerParams(
            collective_id=0, has_side_effects=True, vmem_limit_bytes=48 * 1024 * 1024
        ),
    )(tiles, ids, band_width)


def solution(mesh):
    in_specs = (P("ev", "blk", None, None, None), P("ev", "blk", None), P())
    out_specs = P(None, None, ("ev", "blk"))
    return jax.shard_map(shards, mesh=mesh, in_specs=in_specs, out_specs=out_specs, check_vma=False)
```

```python
import functools

import jax
import jax.numpy as jnp
from jax import lax
from jax.experimental import pallas as pl
from jax.experimental.pallas import tpu as pltpu
from jax.sharding import PartitionSpec as P

NT = 4
CAP = 2
LAYERS = 8
LANES = 128
TAG = 16
MESH = pl.DeviceIdType.MESH


def log2(n):
    assert n & (n - 1) == 0
    return n.bit_length() - 1


def spread_smoother(band, depth, slabs, cols, block):
    shape = (cols * depth, slabs * block)
    row = lax.broadcasted_iota(jnp.int32, shape, 0)
    col = lax.broadcasted_iota(jnp.int32, shape, 1)
    level = row & (depth - 1)
    within = col & (block - 1)
    levels = depth // slabs
    source = (col >> log2(block)) * levels + (within >> log2(cols))
    layer = level >> log2(depth // LAYERS)
    half = jnp.zeros(shape, jnp.int32)
    for n in range(LAYERS):
        half = jnp.where(layer == n, band[n], half)
    weight = jnp.maximum(half + 1 - jnp.abs(level - source), 0)
    weight = jnp.where(within < levels * cols, weight, 0).astype(jnp.float32)
    total = jnp.sum(weight, axis=1, keepdims=True) * (1.0 / cols)
    same = (row >> log2(depth)) == (within & (cols - 1))
    return jnp.where(same, weight / total, 0.0).astype(jnp.bfloat16)


def kernel(dims, tiles_hbm, region_hbm, band_hbm, out_ref, tiles, region, band, spread, pack, land, stage, grad,
           weights, in_sem, send1, recv1, send2, recv2):
    groups, slabs, count, levels, parts, cols, block = dims
    assert groups & (groups - 1) == 0 and slabs & (slabs - 1) == 0
    depth = levels * slabs
    per_tile = slabs // NT
    rows = levels * parts
    me, mine = lax.axis_index("ev"), lax.axis_index("blk")
    peers = [me ^ j for j in range(groups)]
    mates = [mine ^ j for j in range(slabs)]

    loads = [
        pltpu.make_async_copy(region_hbm, region, in_sem.at[0]),
        pltpu.make_async_copy(tiles_hbm, tiles, in_sem.at[1]),
        pltpu.make_async_copy(band_hbm, band, in_sem.at[2]),
    ]
    for load in loads:
        load.start()
    barrier = pltpu.get_barrier_semaphore()
    for j in range(1, groups):
        pl.semaphore_signal(barrier, inc=1, device_id=(peers[j], mine), device_id_type=MESH)
    for j in range(1, slabs):
        pl.semaphore_signal(barrier, inc=1, device_id=(me, mates[j]), device_id_type=MESH)
    loads[0].wait()
    ids = [region[k] for k in range(count)]
    loads[1].wait()

    def pack_section(j):
        first, last = jnp.int32(-1), jnp.int32(-1)
        for k in range(count):
            here = (ids[k] >> log2(NT)) == peers[j]
            last = jnp.where(here, k, last)
            first = jnp.where(here & (first < 0), k, first)
        for slot, (entry, there) in enumerate(((first, first >= 0), (last, last != first))):
            entry = jnp.maximum(entry, 0)
            tile = jnp.where(there, region[entry] & (NT - 1), -1)
            pack[0, j, slot * 8 : slot * 8 + 8, :] = jnp.full((8, LANES), tile, jnp.int32).astype(jnp.bfloat16)
            values = tiles[entry].astype(jnp.float32)
            for k in range(parts):
                spread[j, slot, :, k, :] = values[:, k * LANES : (k + 1) * LANES]
            for c in range(3):
                piece = spread[j, slot, c * levels : (c + 1) * levels].reshape(rows, LANES)
                at = TAG + slot * rows
                pack[c, j, at : at + rows, :] = piece.astype(jnp.bfloat16)

    def send_section(c, j):
        at = pl.ds(0, TAG + CAP * rows) if c == 0 else pl.ds(TAG, CAP * rows)
        copy = pltpu.make_async_remote_copy(
            src_ref=pack.at[c, j, at],
            dst_ref=land.at[c, j, at],
            send_sem=send1.at[c, j],
            recv_sem=recv1.at[c, j],
            device_id=(peers[j], mine),
            device_id_type=MESH,
        )
        copy.start()
        return copy

    def send_columns(c, j):
        copy = pltpu.make_async_remote_copy(
            src_ref=stage.at[c, mates[j]],
            dst_ref=grad.at[c, mine],
            send_sem=send2.at[c, j],
            recv_sem=recv2.at[c, j],
            device_id=(me, mates[j]),
            device_id_type=MESH,
        )
        copy.start()
        return copy

    order = list(range(groups - 1, 0, -1))
    sections, columns = {}, {}
    for n, j in enumerate(order):
        pack_section(j)
        if n == 0:
            pl.semaphore_wait(barrier, groups + slabs - 2)
        sections[0, j] = send_section(0, j)
    for c in range(1, 3):
        for j in order:
            sections[c, j] = send_section(c, j)
    pack_section(0)
    loads[2].wait()
    weights[...] = spread_smoother(band, depth, slabs, cols, block)

    for c in range(3):
        sums = [jnp.zeros((levels * parts // 8, 8, LANES), jnp.float32) for _ in range(NT)]
        for j in range(groups):
            if j > 0:
                sections[c, j].wait_recv()
            held = pack if j == 0 else land
            tags = held[0, j, :TAG, :].astype(jnp.float32)
            for slot in range(CAP):
                at = TAG + slot * rows
                term = held[c, j, at : at + rows, :].astype(jnp.float32).reshape(rows // 8, 8, LANES)
                tag = tags[slot * 8 : slot * 8 + 8]
                for t in range(NT):
                    sums[t] += jnp.where((tag == t)[None], term, 0.0)
        for t in range(NT):
            total = sums[t].reshape(levels, parts, LANES)
            for q in range(per_tile):
                piece = total[:, q * cols : (q + 1) * cols, :].reshape(levels * cols, LANES)
                if block > levels * cols:
                    fill = jnp.zeros((block - levels * cols, LANES), jnp.float32)
                    piece = jnp.concatenate([piece, fill], axis=0)
                stage[c, t * per_tile + q] = piece.astype(jnp.bfloat16)
        for j in range(1, slabs):
            columns[c, j] = send_columns(c, j)
        grad[c, mine] = stage[c, mine]

    for c in range(3):
        for j in range(1, slabs):
            columns[c, j].wait_recv()
        gathered = grad[c].reshape(slabs * block, LANES)
        smooth = jnp.dot(weights[...], gathered, preferred_element_type=jnp.float32)
        for k in range(cols):
            out_ref[c, :, k * LANES : (k + 1) * LANES] = smooth[k * depth : (k + 1) * depth]
    for copy in list(sections.values()) + list(columns.values()):
        copy.wait_send()


def shards(kernel_tiles, region, band_width):
    tiles, ids = kernel_tiles[0, 0], region[0, 0]
    groups, slabs = lax.axis_size("ev"), lax.axis_size("blk")
    count, held, width = tiles.shape
    levels = held // 3
    depth = levels * slabs
    parts = width // LANES
    cols = NT * parts // slabs
    block = -(-levels * cols // 16) * 16
    dims = (groups, slabs, count, levels, parts, cols, block)
    rows = levels * parts
    message = TAG + CAP * rows
    return pl.pallas_call(
        functools.partial(kernel, dims),
        out_shape=jax.ShapeDtypeStruct((3, depth, cols * LANES), jnp.float32),
        in_specs=[pl.BlockSpec(memory_space=pltpu.HBM)] * 3,
        out_specs=pl.BlockSpec(memory_space=pltpu.VMEM),
        scratch_shapes=[
            pltpu.VMEM(tiles.shape, jnp.bfloat16),
            pltpu.SMEM(ids.shape, jnp.int32),
            pltpu.SMEM(band_width.shape, jnp.int32),
            pltpu.VMEM((groups, CAP, held, parts, LANES), jnp.float32),
            pltpu.VMEM((3, groups, message, LANES), jnp.bfloat16),
            pltpu.VMEM((3, groups, message, LANES), jnp.bfloat16),
            pltpu.VMEM((3, slabs, block, LANES), jnp.bfloat16),
            pltpu.VMEM((3, slabs, block, LANES), jnp.bfloat16),
            pltpu.VMEM((cols * depth, slabs * block), jnp.bfloat16),
            pltpu.SemaphoreType.DMA((3,)),
            pltpu.SemaphoreType.DMA((3, groups)),
            pltpu.SemaphoreType.DMA((3, groups)),
            pltpu.SemaphoreType.DMA((3, slabs)),
            pltpu.SemaphoreType.DMA((3, slabs)),
        ],
        compiler_params=pltpu.CompilerParams(
            collective_id=0, has_side_effects=True, vmem_limit_bytes=60 * 1024 * 1024
        ),
    )(tiles, ids, band_width)


def solution(mesh):
    in_specs = (P("ev", "blk", None, None, None), P("ev", "blk", None), P())
    out_specs = P(None, None, ("ev", "blk"))
    return jax.shard_map(shards, mesh=mesh, in_specs=in_specs, out_specs=out_specs, check_vma=False)
```

```python
import functools

import jax
import jax.numpy as jnp
from jax import lax
from jax.experimental import pallas as pl
from jax.experimental.pallas import tpu as pltpu
from jax.sharding import PartitionSpec as P

NT = 4
CAP = 2
LAYERS = 8
LANES = 128
TAG = 16
MESH = pl.DeviceIdType.MESH


def log2(n):
    assert n & (n - 1) == 0
    return n.bit_length() - 1


def spread_smoother(band, depth, slabs, cols, block):
    shape = (cols * depth, slabs * block)
    row = lax.broadcasted_iota(jnp.int32, shape, 0)
    col = lax.broadcasted_iota(jnp.int32, shape, 1)
    level = row & (depth - 1)
    within = col & (block - 1)
    levels = depth // slabs
    source = (col >> log2(block)) * levels + (within >> log2(cols))
    layer = level >> log2(depth // LAYERS)
    half = jnp.zeros(shape, jnp.int32)
    for n in range(LAYERS):
        half = jnp.where(layer == n, band[n], half)
    weight = jnp.maximum(half + 1 - jnp.abs(level - source), 0)
    weight = jnp.where(within < levels * cols, weight, 0).astype(jnp.float32)
    total = jnp.sum(weight, axis=1, keepdims=True) * (1.0 / cols)
    same = (row >> log2(depth)) == (within & (cols - 1))
    return jnp.where(same, weight / total, 0.0).astype(jnp.bfloat16)


def kernel(dims, tiles_hbm, region_hbm, band_hbm, out_ref, tiles, region, band, spread, pack, land, stage, grad,
           weights, in_sem, send1, recv1, send2, recv2):
    groups, slabs, count, levels, parts, cols, block = dims
    assert groups & (groups - 1) == 0 and slabs & (slabs - 1) == 0
    depth = levels * slabs
    per_tile = slabs // NT
    rows = levels * parts
    me, mine = lax.axis_index("ev"), lax.axis_index("blk")
    peers = [me ^ j for j in range(groups)]
    mates = [mine ^ j for j in range(slabs)]

    loads = [
        pltpu.make_async_copy(region_hbm, region, in_sem.at[0]),
        pltpu.make_async_copy(tiles_hbm, tiles, in_sem.at[1]),
        pltpu.make_async_copy(band_hbm, band, in_sem.at[2]),
    ]
    for load in loads:
        load.start()
    barrier = pltpu.get_barrier_semaphore()
    for j in range(1, groups):
        pl.semaphore_signal(barrier, inc=1, device_id=(peers[j], mine), device_id_type=MESH)
    for j in range(1, slabs):
        pl.semaphore_signal(barrier, inc=1, device_id=(me, mates[j]), device_id_type=MESH)
    loads[0].wait()
    ids = [region[k] for k in range(count)]
    loads[1].wait()

    def pack_section(j):
        first, last = jnp.int32(-1), jnp.int32(-1)
        for k in range(count):
            here = (ids[k] >> log2(NT)) == peers[j]
            last = jnp.where(here, k, last)
            first = jnp.where(here & (first < 0), k, first)
        for slot, (entry, there) in enumerate(((first, first >= 0), (last, last != first))):
            entry = jnp.maximum(entry, 0)
            tile = jnp.where(there, region[entry] & (NT - 1), -1)
            pack[0, j, slot * 8 : slot * 8 + 8, :] = jnp.full((8, LANES), tile, jnp.int32).astype(jnp.bfloat16)
            values = tiles[entry].astype(jnp.float32)
            for k in range(parts):
                spread[j, slot, :, k, :] = values[:, k * LANES : (k + 1) * LANES]
            for c in range(3):
                piece = spread[j, slot, c * levels : (c + 1) * levels].reshape(rows, LANES)
                at = TAG + slot * rows
                pack[c, j, at : at + rows, :] = piece.astype(jnp.bfloat16)

    def send_section(c, j):
        at = pl.ds(0, TAG + CAP * rows) if c == 0 else pl.ds(TAG, CAP * rows)
        copy = pltpu.make_async_remote_copy(
            src_ref=pack.at[c, j, at],
            dst_ref=land.at[c, j, at],
            send_sem=send1.at[c, j],
            recv_sem=recv1.at[c, j],
            device_id=(peers[j], mine),
            device_id_type=MESH,
        )
        copy.start()
        return copy

    def send_columns(c, j):
        copy = pltpu.make_async_remote_copy(
            src_ref=stage.at[c, mates[j]],
            dst_ref=grad.at[c, mine],
            send_sem=send2.at[c, j],
            recv_sem=recv2.at[c, j],
            device_id=(me, mates[j]),
            device_id_type=MESH,
        )
        copy.start()
        return copy

    order = list(range(groups - 1, 0, -1))
    sections, columns = {}, {}
    for n, j in enumerate(order):
        pack_section(j)
        if n == 0:
            pl.semaphore_wait(barrier, groups + slabs - 2)
        sections[0, j] = send_section(0, j)
    for c in range(1, 3):
        for j in order:
            sections[c, j] = send_section(c, j)
    pack_section(0)
    loads[2].wait()
    weights[...] = spread_smoother(band, depth, slabs, cols, block)

    for c in range(3):
        sums = [jnp.zeros((levels * parts // 8, 8, LANES), jnp.float32) for _ in range(NT)]
        for j in range(groups):
            if j > 0:
                sections[c, j].wait_recv()
            held = pack if j == 0 else land
            tags = held[0, j, :TAG, :].astype(jnp.float32)
            for slot in range(CAP):
                at = TAG + slot * rows
                term = held[c, j, at : at + rows, :].astype(jnp.float32).reshape(rows // 8, 8, LANES)
                tag = tags[slot * 8 : slot * 8 + 8]
                for t in range(NT):
                    sums[t] += jnp.where((tag == t)[None], term, 0.0)
        for t in range(NT):
            total = sums[t].reshape(levels, parts, LANES)
            for q in range(per_tile):
                piece = total[:, q * cols : (q + 1) * cols, :].reshape(levels * cols, LANES)
                if block > levels * cols:
                    fill = jnp.zeros((block - levels * cols, LANES), jnp.float32)
                    piece = jnp.concatenate([piece, fill], axis=0)
                stage[c, t * per_tile + q] = piece.astype(jnp.bfloat16)
        for j in range(1, slabs):
            columns[c, j] = send_columns(c, j)
        grad[c, mine] = stage[c, mine]

    for c in range(3):
        for j in range(1, slabs):
            columns[c, j].wait_recv()
        gathered = grad[c].reshape(slabs * block, LANES)
        smooth = jnp.dot(weights[...], gathered, preferred_element_type=jnp.float32)
        for k in range(cols):
            out_ref[c, :, k * LANES : (k + 1) * LANES] = smooth[k * depth : (k + 1) * depth]
    for copy in list(sections.values()) + list(columns.values()):
        copy.wait_send()


def shards(kernel_tiles, region, band_width):
    tiles, ids = kernel_tiles[0, 0], region[0, 0]
    groups, slabs = lax.axis_size("ev"), lax.axis_size("blk")
    count, held, width = tiles.shape
    levels = held // 3
    depth = levels * slabs
    parts = width // LANES
    cols = NT * parts // slabs
    block = -(-levels * cols // 16) * 16
    dims = (groups, slabs, count, levels, parts, cols, block)
    rows = levels * parts
    message = TAG + CAP * rows
    return pl.pallas_call(
        functools.partial(kernel, dims),
        out_shape=pltpu.VMEM((3, depth, cols * LANES), jnp.float32),
        in_specs=[pl.BlockSpec(memory_space=pltpu.HBM)] * 3,
        out_specs=pl.BlockSpec(memory_space=pltpu.VMEM),
        scratch_shapes=[
            pltpu.VMEM(tiles.shape, jnp.bfloat16),
            pltpu.SMEM(ids.shape, jnp.int32),
            pltpu.SMEM(band_width.shape, jnp.int32),
            pltpu.VMEM((groups, CAP, held, parts, LANES), jnp.float32),
            pltpu.VMEM((3, groups, message, LANES), jnp.bfloat16),
            pltpu.VMEM((3, groups, message, LANES), jnp.bfloat16),
            pltpu.VMEM((3, slabs, block, LANES), jnp.bfloat16),
            pltpu.VMEM((3, slabs, block, LANES), jnp.bfloat16),
            pltpu.VMEM((cols * depth, slabs * block), jnp.bfloat16),
            pltpu.SemaphoreType.DMA((3,)),
            pltpu.SemaphoreType.DMA((3, groups)),
            pltpu.SemaphoreType.DMA((3, groups)),
            pltpu.SemaphoreType.DMA((3, slabs)),
            pltpu.SemaphoreType.DMA((3, slabs)),
        ],
        compiler_params=pltpu.CompilerParams(
            collective_id=0, has_side_effects=True, vmem_limit_bytes=48 * 1024 * 1024
        ),
    )(*[pltpu.with_memory_space_constraint(a, pltpu.HBM) for a in (tiles, ids, band_width)])


def solution(mesh):
    in_specs = (P("ev", "blk", None, None, None), P("ev", "blk", None), P())
    out_specs = P(None, None, ("ev", "blk"))
    return jax.shard_map(shards, mesh=mesh, in_specs=in_specs, out_specs=out_specs, check_vma=False)
```

```python
import functools

import jax
import jax.numpy as jnp
from jax import lax
from jax.experimental import pallas as pl
from jax.experimental.pallas import tpu as pltpu
from jax.sharding import PartitionSpec as P

NT = 4
CAP = 2
LAYERS = 8
LANES = 128
MESH = pl.DeviceIdType.MESH


def log2(n):
    assert n & (n - 1) == 0
    return n.bit_length() - 1


def spread_smoother(band, depth, slabs, cols, block):
    shape = (cols * depth, slabs * block)
    row = lax.broadcasted_iota(jnp.int32, shape, 0)
    col = lax.broadcasted_iota(jnp.int32, shape, 1)
    level = row & (depth - 1)
    within = col & (block - 1)
    levels = depth // slabs
    source = (col >> log2(block)) * levels + (within >> log2(cols))
    layer = level >> log2(depth // LAYERS)
    half = jnp.zeros(shape, jnp.int32)
    for n in range(LAYERS):
        half = jnp.where(layer == n, band[n], half)
    weight = jnp.maximum(half + 1 - jnp.abs(level - source), 0)
    weight = jnp.where(within < levels * cols, weight, 0).astype(jnp.float32)
    total = jnp.sum(weight, axis=1, keepdims=True) * (1.0 / cols)
    same = (row >> log2(depth)) == (within & (cols - 1))
    return jnp.where(same, weight / total, 0.0).astype(jnp.bfloat16)


def kernel(dims, tiles_hbm, region_hbm, band_hbm, out_ref, tiles, region, band, spread, tags, tags_in, pack, land,
           stage, grad, weights, in_sem, send0, recv0, send1, recv1, send2, recv2):
    groups, slabs, count, levels, parts, cols, block = dims
    assert groups & (groups - 1) == 0 and slabs & (slabs - 1) == 0
    depth = levels * slabs
    per_tile = slabs // NT
    rows = levels * parts
    me, mine = lax.axis_index("ev"), lax.axis_index("blk")
    peers = [me ^ j for j in range(groups)]
    mates = [mine ^ j for j in range(slabs)]

    loads = [
        pltpu.make_async_copy(region_hbm, region, in_sem.at[0]),
        pltpu.make_async_copy(tiles_hbm, tiles, in_sem.at[1]),
        pltpu.make_async_copy(band_hbm, band, in_sem.at[2]),
    ]
    for load in loads:
        load.start()
    barrier = pltpu.get_barrier_semaphore()
    for j in range(1, groups):
        pl.semaphore_signal(barrier, inc=1, device_id=(peers[j], mine), device_id_type=MESH)
    for j in range(1, slabs):
        pl.semaphore_signal(barrier, inc=1, device_id=(me, mates[j]), device_id_type=MESH)
    loads[0].wait()
    ids = [region[k] for k in range(count)]

    def find(j):
        first, last = jnp.int32(-1), jnp.int32(-1)
        for k in range(count):
            here = (ids[k] >> log2(NT)) == peers[j]
            last = jnp.where(here, k, last)
            first = jnp.where(here & (first < 0), k, first)
        entries = [jnp.maximum(first, 0), jnp.maximum(last, 0)]
        for slot, there in enumerate((first >= 0, last != first)):
            tile = jnp.where(there, region[entries[slot]] & (NT - 1), -1)
            tags[j, slot : slot + 1, :] = jnp.full((1, LANES), tile, jnp.int32)
        return entries

    def pack_section(j, entries):
        for slot, entry in enumerate(entries):
            values = tiles[entry].astype(jnp.float32)
            held = 3 * levels
            for k in range(parts):
                spread[j, slot, pl.ds(k, held, stride=parts), :] = values[:, k * LANES : (k + 1) * LANES]
            for c in range(3):
                piece = spread[j, slot, c * rows : (c + 1) * rows, :]
                pack[c, j, slot * rows : (slot + 1) * rows, :] = piece.astype(jnp.bfloat16)

    def send_tags(j):
        copy = pltpu.make_async_remote_copy(
            src_ref=tags.at[j],
            dst_ref=tags_in.at[j],
            send_sem=send0.at[j],
            recv_sem=recv0.at[j],
            device_id=(peers[j], mine),
            device_id_type=MESH,
        )
        copy.start()
        return copy

    def send_section(c, j):
        copy = pltpu.make_async_remote_copy(
            src_ref=pack.at[c, j],
            dst_ref=land.at[c, j],
            send_sem=send1.at[c, j],
            recv_sem=recv1.at[c, j],
            device_id=(peers[j], mine),
            device_id_type=MESH,
        )
        copy.start()
        return copy

    def send_columns(c, j):
        copy = pltpu.make_async_remote_copy(
            src_ref=stage.at[c, mates[j]],
            dst_ref=grad.at[c, mine],
            send_sem=send2.at[c, j],
            recv_sem=recv2.at[c, j],
            device_id=(me, mates[j]),
            device_id_type=MESH,
        )
        copy.start()
        return copy

    order = list(range(groups - 1, 0, -1))
    entries = [find(j) for j in range(groups)]
    pl.semaphore_wait(barrier, groups + slabs - 2)
    numbers = {j: send_tags(j) for j in order}
    loads[1].wait()
    sections, columns = {}, {}
    for j in order:
        pack_section(j, entries[j])
        sections[0, j] = send_section(0, j)
    for c in range(1, 3):
        for j in order:
            sections[c, j] = send_section(c, j)
    pack_section(0, entries[0])
    loads[2].wait()
    weights[...] = spread_smoother(band, depth, slabs, cols, block)

    for c in range(3):
        sums = [jnp.zeros((rows // 8, 8, LANES), jnp.float32) for _ in range(NT)]
        for j in range(groups):
            if j > 0:
                if c == 0:
                    numbers[j].wait_recv()
                sections[c, j].wait_recv()
            held = pack if j == 0 else land
            number = tags[j] if j == 0 else tags_in[j]
            for slot in range(CAP):
                term = held[c, j, slot * rows : (slot + 1) * rows, :].astype(jnp.float32)
                term = term.reshape(rows // 8, 8, LANES)
                tag = jnp.broadcast_to(number[slot : slot + 1], (8, LANES))
                for t in range(NT):
                    sums[t] += jnp.where((tag == t)[None], term, 0.0)
        for t in range(NT):
            total = sums[t].reshape(levels, parts, LANES)
            for q in range(per_tile):
                piece = total[:, q * cols : (q + 1) * cols, :].reshape(levels * cols, LANES)
                if block > levels * cols:
                    fill = jnp.zeros((block - levels * cols, LANES), jnp.float32)
                    piece = jnp.concatenate([piece, fill], axis=0)
                stage[c, t * per_tile + q] = piece.astype(jnp.bfloat16)
        for j in range(1, slabs):
            columns[c, j] = send_columns(c, j)
        grad[c, mine] = stage[c, mine]

    for c in range(3):
        for j in range(1, slabs):
            columns[c, j].wait_recv()
        gathered = grad[c].reshape(slabs * block, LANES)
        smooth = jnp.dot(weights[...], gathered, preferred_element_type=jnp.float32)
        for k in range(cols):
            out_ref[c, :, k * LANES : (k + 1) * LANES] = smooth[k * depth : (k + 1) * depth]
    for copy in [*numbers.values(), *sections.values(), *columns.values()]:
        copy.wait_send()


def shards(kernel_tiles, region, band_width):
    tiles, ids = kernel_tiles[0, 0], region[0, 0]
    groups, slabs = lax.axis_size("ev"), lax.axis_size("blk")
    count, held, width = tiles.shape
    levels = held // 3
    depth = levels * slabs
    parts = width // LANES
    cols = NT * parts // slabs
    block = -(-levels * cols // 16) * 16
    dims = (groups, slabs, count, levels, parts, cols, block)
    rows = levels * parts
    message = CAP * rows
    return pl.pallas_call(
        functools.partial(kernel, dims),
        out_shape=pltpu.VMEM((3, depth, cols * LANES), jnp.float32),
        in_specs=[pl.BlockSpec(memory_space=pltpu.HBM)] * 3,
        out_specs=pl.BlockSpec(memory_space=pltpu.VMEM),
        scratch_shapes=[
            pltpu.VMEM(tiles.shape, jnp.bfloat16),
            pltpu.SMEM(ids.shape, jnp.int32),
            pltpu.SMEM(band_width.shape, jnp.int32),
            pltpu.VMEM((groups, CAP, held * parts, LANES), jnp.float32),
            pltpu.VMEM((groups, CAP, LANES), jnp.int32),
            pltpu.VMEM((groups, CAP, LANES), jnp.int32),
            pltpu.VMEM((3, groups, message, LANES), jnp.bfloat16),
            pltpu.VMEM((3, groups, message, LANES), jnp.bfloat16),
            pltpu.VMEM((3, slabs, block, LANES), jnp.bfloat16),
            pltpu.VMEM((3, slabs, block, LANES), jnp.bfloat16),
            pltpu.VMEM((cols * depth, slabs * block), jnp.bfloat16),
            pltpu.SemaphoreType.DMA((3,)),
            pltpu.SemaphoreType.DMA((groups,)),
            pltpu.SemaphoreType.DMA((groups,)),
            pltpu.SemaphoreType.DMA((3, groups)),
            pltpu.SemaphoreType.DMA((3, groups)),
            pltpu.SemaphoreType.DMA((3, slabs)),
            pltpu.SemaphoreType.DMA((3, slabs)),
        ],
        compiler_params=pltpu.CompilerParams(
            collective_id=0, has_side_effects=True, vmem_limit_bytes=48 * 1024 * 1024
        ),
    )(*[pltpu.with_memory_space_constraint(a, pltpu.HBM) for a in (tiles, ids, band_width)])


def solution(mesh):
    in_specs = (P("ev", "blk", None, None, None), P("ev", "blk", None), P())
    out_specs = P(None, None, ("ev", "blk"))
    return jax.shard_map(shards, mesh=mesh, in_specs=in_specs, out_specs=out_specs, check_vma=False)
```

```python
import functools

import jax
import jax.numpy as jnp
from jax import lax
from jax.experimental import pallas as pl
from jax.experimental.pallas import tpu as pltpu
from jax.sharding import PartitionSpec as P

NT = 4
CAP = 2
LAYERS = 8
LANES = 128
MESH = pl.DeviceIdType.MESH


def log2(n):
    assert n & (n - 1) == 0
    return n.bit_length() - 1


def spread_smoother(band, depth, slabs, cols, block):
    shape = (cols * depth, slabs * block)
    row = lax.broadcasted_iota(jnp.int32, shape, 0)
    col = lax.broadcasted_iota(jnp.int32, shape, 1)
    level = row & (depth - 1)
    within = col & (block - 1)
    levels = depth // slabs
    source = (col >> log2(block)) * levels + (within >> log2(cols))
    layer = level >> log2(depth // LAYERS)
    half = jnp.zeros(shape, jnp.int32)
    for n in range(LAYERS):
        half = jnp.where(layer == n, band[n], half)
    weight = jnp.maximum(half + 1 - jnp.abs(level - source), 0)
    weight = jnp.where(within < levels * cols, weight, 0).astype(jnp.float32)
    total = jnp.sum(weight, axis=1, keepdims=True) * (1.0 / cols)
    same = (row >> log2(depth)) == (within & (cols - 1))
    return jnp.where(same, weight / total, 0.0).astype(jnp.bfloat16)


def kernel(dims, tiles_hbm, region_hbm, band_hbm, out_ref, tiles, region, band, spread, tags, tags_in, pack, land,
           stage, grad, weights, in_sem, send0, recv0, send1, recv1, send2, recv2):
    groups, slabs, count, levels, parts, cols, block = dims
    assert groups & (groups - 1) == 0 and slabs & (slabs - 1) == 0
    depth = levels * slabs
    per_tile = slabs // NT
    rows = levels * parts
    me, mine = lax.axis_index("ev"), lax.axis_index("blk")
    peers = [me ^ j for j in range(groups)]
    mates = [mine ^ j for j in range(slabs)]

    loads = [
        pltpu.make_async_copy(region_hbm, region, in_sem.at[0]),
        pltpu.make_async_copy(tiles_hbm, tiles, in_sem.at[1]),
        pltpu.make_async_copy(band_hbm, band, in_sem.at[2]),
    ]
    for load in loads:
        load.start()
    barrier = pltpu.get_barrier_semaphore()
    for j in range(1, groups):
        pl.semaphore_signal(barrier, inc=1, device_id=(peers[j], mine), device_id_type=MESH)
    for j in range(1, slabs):
        pl.semaphore_signal(barrier, inc=1, device_id=(me, mates[j]), device_id_type=MESH)
    loads[0].wait()
    ids = [region[k] for k in range(count)]

    def find(j):
        first, last = jnp.int32(-1), jnp.int32(-1)
        for k in range(count):
            here = (ids[k] >> log2(NT)) == peers[j]
            last = jnp.where(here, k, last)
            first = jnp.where(here & (first < 0), k, first)
        entries = [jnp.maximum(first, 0), jnp.maximum(last, 0)]
        for slot, there in enumerate((first >= 0, last != first)):
            tile = jnp.where(there, region[entries[slot]] & (NT - 1), -1)
            tags[j, slot : slot + 1, :] = jnp.full((1, LANES), tile, jnp.int32)
        return entries

    def pack_section(j, entries):
        for slot, entry in enumerate(entries):
            values = tiles[entry].astype(jnp.float32)
            held = 3 * levels
            for k in range(parts):
                spread[j, slot, pl.ds(k, held, stride=parts), :] = values[:, k * LANES : (k + 1) * LANES]
            for c in range(3):
                piece = spread[j, slot, c * rows : (c + 1) * rows, :]
                pack[c, j, slot * rows : (slot + 1) * rows, :] = piece.astype(jnp.bfloat16)

    def send_tags(j):
        copy = pltpu.make_async_remote_copy(
            src_ref=tags.at[j],
            dst_ref=tags_in.at[j],
            send_sem=send0.at[j],
            recv_sem=recv0.at[j],
            device_id=(peers[j], mine),
            device_id_type=MESH,
        )
        copy.start()
        return copy

    def send_section(c, j):
        copy = pltpu.make_async_remote_copy(
            src_ref=pack.at[c, j],
            dst_ref=land.at[c, j],
            send_sem=send1.at[c, j],
            recv_sem=recv1.at[c, j],
            device_id=(peers[j], mine),
            device_id_type=MESH,
        )
        copy.start()
        return copy

    def send_columns(c, j):
        copy = pltpu.make_async_remote_copy(
            src_ref=stage.at[c, mates[j]],
            dst_ref=grad.at[c, mine],
            send_sem=send2.at[c, j],
            recv_sem=recv2.at[c, j],
            device_id=(me, mates[j]),
            device_id_type=MESH,
        )
        copy.start()
        return copy

    order = list(range(groups - 1, 0, -1))
    entries = [find(j) for j in range(groups)]
    pl.semaphore_wait(barrier, groups + slabs - 2)
    numbers = {j: send_tags(j) for j in order}
    loads[1].wait()
    sections, columns = {}, {}
    for j in order:
        pack_section(j, entries[j])
        sections[0, j] = send_section(0, j)
    pack_section(0, entries[0])
    loads[2].wait()
    weights[...] = spread_smoother(band, depth, slabs, cols, block)

    def send_next(c):
        for j in order:
            sections[c - 1, j].wait_send()
            sections[c, j] = send_section(c, j)

    send_next(1)
    for c in range(3):
        sums = [jnp.zeros((rows // 8, 8, LANES), jnp.float32) for _ in range(NT)]
        for j in range(groups):
            if j > 0:
                if c == 0:
                    numbers[j].wait_recv()
                sections[c, j].wait_recv()
            held = pack if j == 0 else land
            number = tags[j] if j == 0 else tags_in[j]
            for slot in range(CAP):
                term = held[c, j, slot * rows : (slot + 1) * rows, :].astype(jnp.float32)
                term = term.reshape(rows // 8, 8, LANES)
                tag = jnp.broadcast_to(number[slot : slot + 1], (8, LANES))
                for t in range(NT):
                    sums[t] += jnp.where((tag == t)[None], term, 0.0)
        for t in range(NT):
            total = sums[t].reshape(levels, parts, LANES)
            for q in range(per_tile):
                piece = total[:, q * cols : (q + 1) * cols, :].reshape(levels * cols, LANES)
                if block > levels * cols:
                    fill = jnp.zeros((block - levels * cols, LANES), jnp.float32)
                    piece = jnp.concatenate([piece, fill], axis=0)
                stage[c, t * per_tile + q] = piece.astype(jnp.bfloat16)
        for j in range(1, slabs):
            columns[c, j] = send_columns(c, j)
        grad[c, mine] = stage[c, mine]
        if c == 0:
            send_next(2)

    for c in range(3):
        for j in range(1, slabs):
            columns[c, j].wait_recv()
        gathered = grad[c].reshape(slabs * block, LANES)
        smooth = jnp.dot(weights[...], gathered, preferred_element_type=jnp.float32)
        for k in range(cols):
            out_ref[c, :, k * LANES : (k + 1) * LANES] = smooth[k * depth : (k + 1) * depth]
    for copy in [*numbers.values(), *(sections[2, j] for j in order), *columns.values()]:
        copy.wait_send()


def shards(kernel_tiles, region, band_width):
    tiles, ids = kernel_tiles[0, 0], region[0, 0]
    groups, slabs = lax.axis_size("ev"), lax.axis_size("blk")
    count, held, width = tiles.shape
    levels = held // 3
    depth = levels * slabs
    parts = width // LANES
    cols = NT * parts // slabs
    block = -(-levels * cols // 16) * 16
    dims = (groups, slabs, count, levels, parts, cols, block)
    rows = levels * parts
    message = CAP * rows
    return pl.pallas_call(
        functools.partial(kernel, dims),
        out_shape=pltpu.VMEM((3, depth, cols * LANES), jnp.float32),
        in_specs=[pl.BlockSpec(memory_space=pltpu.HBM)] * 3,
        out_specs=pl.BlockSpec(memory_space=pltpu.VMEM),
        scratch_shapes=[
            pltpu.VMEM(tiles.shape, jnp.bfloat16),
            pltpu.SMEM(ids.shape, jnp.int32),
            pltpu.SMEM(band_width.shape, jnp.int32),
            pltpu.VMEM((groups, CAP, held * parts, LANES), jnp.float32),
            pltpu.VMEM((groups, CAP, LANES), jnp.int32),
            pltpu.VMEM((groups, CAP, LANES), jnp.int32),
            pltpu.VMEM((3, groups, message, LANES), jnp.bfloat16),
            pltpu.VMEM((3, groups, message, LANES), jnp.bfloat16),
            pltpu.VMEM((3, slabs, block, LANES), jnp.bfloat16),
            pltpu.VMEM((3, slabs, block, LANES), jnp.bfloat16),
            pltpu.VMEM((cols * depth, slabs * block), jnp.bfloat16),
            pltpu.SemaphoreType.DMA((3,)),
            pltpu.SemaphoreType.DMA((groups,)),
            pltpu.SemaphoreType.DMA((groups,)),
            pltpu.SemaphoreType.DMA((3, groups)),
            pltpu.SemaphoreType.DMA((3, groups)),
            pltpu.SemaphoreType.DMA((3, slabs)),
            pltpu.SemaphoreType.DMA((3, slabs)),
        ],
        compiler_params=pltpu.CompilerParams(
            collective_id=0, has_side_effects=True, vmem_limit_bytes=48 * 1024 * 1024
        ),
    )(*[pltpu.with_memory_space_constraint(a, pltpu.HBM) for a in (tiles, ids, band_width)])


def solution(mesh):
    in_specs = (P("ev", "blk", None, None, None), P("ev", "blk", None), P())
    out_specs = P(None, None, ("ev", "blk"))
    return jax.shard_map(shards, mesh=mesh, in_specs=in_specs, out_specs=out_specs, check_vma=False)
```

```python
import functools

import jax
import jax.numpy as jnp
from jax import lax
from jax.experimental import pallas as pl
from jax.experimental.pallas import tpu as pltpu
from jax.sharding import PartitionSpec as P

NT = 4
CAP = 2
LAYERS = 8
LANES = 128
CHUNKS = ((0, 3),)
MESH = pl.DeviceIdType.MESH


def log2(n):
    assert n & (n - 1) == 0
    return n.bit_length() - 1


def spread_smoother(band, depth, slabs, cols, block):
    shape = (cols * depth, slabs * block)
    row = lax.broadcasted_iota(jnp.int32, shape, 0)
    col = lax.broadcasted_iota(jnp.int32, shape, 1)
    level = row & (depth - 1)
    within = col & (block - 1)
    levels = depth // slabs
    source = (col >> log2(block)) * levels + (within >> log2(cols))
    layer = level >> log2(depth // LAYERS)
    half = jnp.zeros(shape, jnp.int32)
    for n in range(LAYERS):
        half = jnp.where(layer == n, band[n], half)
    weight = jnp.maximum(half + 1 - jnp.abs(level - source), 0)
    weight = jnp.where(within < levels * cols, weight, 0).astype(jnp.float32)
    total = jnp.sum(weight, axis=1, keepdims=True) * (1.0 / cols)
    same = (row >> log2(depth)) == (within & (cols - 1))
    return jnp.where(same, weight / total, 0.0).astype(jnp.bfloat16)


def kernel(dims, tiles_hbm, region_hbm, band_hbm, out_ref, tiles, region, band, spread, tags, tags_in, pack, land,
           stage, grad, weights, in_sem, send0, recv0, send1, recv1, send2, recv2):
    groups, slabs, count, levels, parts, cols, block = dims
    assert groups & (groups - 1) == 0 and slabs & (slabs - 1) == 0
    depth = levels * slabs
    per_tile = slabs // NT
    rows = levels * parts
    me, mine = lax.axis_index("ev"), lax.axis_index("blk")
    peers = [me ^ j for j in range(groups)]
    mates = [mine ^ j for j in range(slabs)]

    loads = [
        pltpu.make_async_copy(region_hbm, region, in_sem.at[0]),
        pltpu.make_async_copy(tiles_hbm, tiles, in_sem.at[1]),
        pltpu.make_async_copy(band_hbm, band, in_sem.at[2]),
    ]
    for load in loads:
        load.start()
    barrier = pltpu.get_barrier_semaphore()
    for j in range(1, groups):
        pl.semaphore_signal(barrier, inc=1, device_id=(peers[j], mine), device_id_type=MESH)
    for j in range(1, slabs):
        pl.semaphore_signal(barrier, inc=1, device_id=(me, mates[j]), device_id_type=MESH)
    loads[0].wait()
    ids = [region[k] for k in range(count)]

    def find(j):
        first, last = jnp.int32(-1), jnp.int32(-1)
        for k in range(count):
            here = (ids[k] >> log2(NT)) == peers[j]
            last = jnp.where(here, k, last)
            first = jnp.where(here & (first < 0), k, first)
        entries = [jnp.maximum(first, 0), jnp.maximum(last, 0)]
        for slot, there in enumerate((first >= 0, last != first)):
            tile = jnp.where(there, region[entries[slot]] & (NT - 1), -1)
            tags[j, slot : slot + 1, :] = jnp.full((1, LANES), tile, jnp.int32)
        return entries

    def pack_section(j, entries):
        for slot, entry in enumerate(entries):
            values = tiles[entry].astype(jnp.float32)
            held = 3 * levels
            for k in range(parts):
                spread[j, slot, pl.ds(k, held, stride=parts), :] = values[:, k * LANES : (k + 1) * LANES]
            for c in range(3):
                piece = spread[j, slot, c * rows : (c + 1) * rows, :]
                pack[j, c, slot * rows : (slot + 1) * rows, :] = piece.astype(jnp.bfloat16)

    def send_tags(j):
        copy = pltpu.make_async_remote_copy(
            src_ref=tags.at[j],
            dst_ref=tags_in.at[j],
            send_sem=send0.at[j],
            recv_sem=recv0.at[j],
            device_id=(peers[j], mine),
            device_id_type=MESH,
        )
        copy.start()
        return copy

    def send_section(n, j):
        copy = pltpu.make_async_remote_copy(
            src_ref=pack.at[j, pl.ds(*CHUNKS[n])],
            dst_ref=land.at[j, pl.ds(*CHUNKS[n])],
            send_sem=send1.at[n, j],
            recv_sem=recv1.at[n, j],
            device_id=(peers[j], mine),
            device_id_type=MESH,
        )
        copy.start()
        return copy

    def send_columns(n, j):
        copy = pltpu.make_async_remote_copy(
            src_ref=stage.at[mates[j], pl.ds(*CHUNKS[n])],
            dst_ref=grad.at[mine, pl.ds(*CHUNKS[n])],
            send_sem=send2.at[n, j],
            recv_sem=recv2.at[n, j],
            device_id=(me, mates[j]),
            device_id_type=MESH,
        )
        copy.start()
        return copy

    order = list(range(groups - 1, 0, -1))
    entries = [find(j) for j in range(groups)]
    pl.semaphore_wait(barrier, groups + slabs - 2)
    numbers = {j: send_tags(j) for j in order}
    loads[1].wait()
    sections, columns = {}, {}
    for j in order:
        pack_section(j, entries[j])
        sections[0, j] = send_section(0, j)
    for n in range(1, len(CHUNKS)):
        for j in order:
            sections[n, j] = send_section(n, j)
    pack_section(0, entries[0])
    loads[2].wait()
    weights[...] = spread_smoother(band, depth, slabs, cols, block)

    def reduce(c, n, first):
        sums = [jnp.zeros((rows // 8, 8, LANES), jnp.float32) for _ in range(NT)]
        for j in range(groups):
            if j > 0 and first:
                if n == 0:
                    numbers[j].wait_recv()
                sections[n, j].wait_recv()
            held = pack if j == 0 else land
            number = tags[j] if j == 0 else tags_in[j]
            for slot in range(CAP):
                term = held[j, c, slot * rows : (slot + 1) * rows, :].astype(jnp.float32)
                term = term.reshape(rows // 8, 8, LANES)
                tag = jnp.broadcast_to(number[slot : slot + 1], (8, LANES))
                for t in range(NT):
                    sums[t] += jnp.where((tag == t)[None], term, 0.0)
        for t in range(NT):
            total = sums[t].reshape(levels, parts, LANES)
            for q in range(per_tile):
                piece = total[:, q * cols : (q + 1) * cols, :].reshape(levels * cols, LANES)
                if block > levels * cols:
                    fill = jnp.zeros((block - levels * cols, LANES), jnp.float32)
                    piece = jnp.concatenate([piece, fill], axis=0)
                stage[t * per_tile + q, c] = piece.astype(jnp.bfloat16)

    for n, (low, size) in enumerate(CHUNKS):
        for c in range(low, low + size):
            reduce(c, n, c == low)
        for j in range(1, slabs):
            columns[n, j] = send_columns(n, j)
        grad[mine, pl.ds(low, size)] = stage[mine, pl.ds(low, size)]

    for n, (low, size) in enumerate(CHUNKS):
        for j in range(1, slabs):
            columns[n, j].wait_recv()
        for c in range(low, low + size):
            gathered = grad[:, c].reshape(slabs * block, LANES)
            smooth = jnp.dot(weights[...], gathered, preferred_element_type=jnp.float32)
            for k in range(cols):
                out_ref[c, :, k * LANES : (k + 1) * LANES] = smooth[k * depth : (k + 1) * depth]
    for copy in [*numbers.values(), *sections.values(), *columns.values()]:
        copy.wait_send()


def shards(kernel_tiles, region, band_width):
    tiles, ids = kernel_tiles[0, 0], region[0, 0]
    groups, slabs = lax.axis_size("ev"), lax.axis_size("blk")
    count, held, width = tiles.shape
    levels = held // 3
    depth = levels * slabs
    parts = width // LANES
    cols = NT * parts // slabs
    block = -(-levels * cols // 16) * 16
    dims = (groups, slabs, count, levels, parts, cols, block)
    rows = levels * parts
    message = CAP * rows
    return pl.pallas_call(
        functools.partial(kernel, dims),
        out_shape=pltpu.VMEM((3, depth, cols * LANES), jnp.float32),
        in_specs=[pl.BlockSpec(memory_space=pltpu.HBM)] * 3,
        out_specs=pl.BlockSpec(memory_space=pltpu.VMEM),
        scratch_shapes=[
            pltpu.VMEM(tiles.shape, jnp.bfloat16),
            pltpu.SMEM(ids.shape, jnp.int32),
            pltpu.SMEM(band_width.shape, jnp.int32),
            pltpu.VMEM((groups, CAP, held * parts, LANES), jnp.float32),
            pltpu.VMEM((groups, CAP, LANES), jnp.int32),
            pltpu.VMEM((groups, CAP, LANES), jnp.int32),
            pltpu.VMEM((groups, 3, message, LANES), jnp.bfloat16),
            pltpu.VMEM((groups, 3, message, LANES), jnp.bfloat16),
            pltpu.VMEM((slabs, 3, block, LANES), jnp.bfloat16),
            pltpu.VMEM((slabs, 3, block, LANES), jnp.bfloat16),
            pltpu.VMEM((cols * depth, slabs * block), jnp.bfloat16),
            pltpu.SemaphoreType.DMA((3,)),
            pltpu.SemaphoreType.DMA((groups,)),
            pltpu.SemaphoreType.DMA((groups,)),
            pltpu.SemaphoreType.DMA((len(CHUNKS), groups)),
            pltpu.SemaphoreType.DMA((len(CHUNKS), groups)),
            pltpu.SemaphoreType.DMA((len(CHUNKS), slabs)),
            pltpu.SemaphoreType.DMA((len(CHUNKS), slabs)),
        ],
        compiler_params=pltpu.CompilerParams(
            collective_id=0, has_side_effects=True, vmem_limit_bytes=48 * 1024 * 1024
        ),
    )(*[pltpu.with_memory_space_constraint(a, pltpu.HBM) for a in (tiles, ids, band_width)])


def solution(mesh):
    in_specs = (P("ev", "blk", None, None, None), P("ev", "blk", None), P())
    out_specs = P(None, None, ("ev", "blk"))
    return jax.shard_map(shards, mesh=mesh, in_specs=in_specs, out_specs=out_specs, check_vma=False)
```

```python
import functools

import jax
import jax.numpy as jnp
from jax import lax
from jax.experimental import pallas as pl
from jax.experimental.pallas import tpu as pltpu
from jax.sharding import PartitionSpec as P

NT = 4
CAP = 2
LAYERS = 8
LANES = 128
CHUNKS = ((0, 3),)
MESH = pl.DeviceIdType.MESH


def log2(n):
    assert n & (n - 1) == 0
    return n.bit_length() - 1


def spread_smoother(band, depth, slabs, cols, block):
    shape = (cols * depth, slabs * block)
    row = lax.broadcasted_iota(jnp.int32, shape, 0)
    col = lax.broadcasted_iota(jnp.int32, shape, 1)
    level = row & (depth - 1)
    within = col & (block - 1)
    levels = depth // slabs
    source = (col >> log2(block)) * levels + (within >> log2(cols))
    layer = level >> log2(depth // LAYERS)
    half = jnp.zeros(shape, jnp.int32)
    for n in range(LAYERS):
        half = jnp.where(layer == n, band[n], half)
    weight = jnp.maximum(half + 1 - jnp.abs(level - source), 0)
    weight = jnp.where(within < levels * cols, weight, 0).astype(jnp.float32)
    total = jnp.sum(weight, axis=1, keepdims=True) * (1.0 / cols)
    same = (row >> log2(depth)) == (within & (cols - 1))
    return jnp.where(same, weight / total, 0.0).astype(jnp.bfloat16)


def kernel(dims, tiles_hbm, region_hbm, band_hbm, out_ref, tiles, region, band, spread, tags, tags_in, pack, land,
           stage, grad, weights, in_sem, send0, recv0, send1, recv1, send2, recv2):
    groups, slabs, count, levels, parts, cols, block = dims
    assert groups & (groups - 1) == 0 and slabs & (slabs - 1) == 0
    depth = levels * slabs
    per_tile = slabs // NT
    rows = levels * parts
    me, mine = lax.axis_index("ev"), lax.axis_index("blk")
    peers = [me ^ j for j in range(groups)]
    mates = [mine ^ j for j in range(slabs)]

    loads = [
        pltpu.make_async_copy(region_hbm, region, in_sem.at[0]),
        pltpu.make_async_copy(tiles_hbm, tiles, in_sem.at[1]),
        pltpu.make_async_copy(band_hbm, band, in_sem.at[2]),
    ]
    for load in loads:
        load.start()
    barrier = pltpu.get_barrier_semaphore()
    for j in range(1, groups):
        pl.semaphore_signal(barrier, inc=1, device_id=(peers[j], mine), device_id_type=MESH)
    for j in range(1, slabs):
        pl.semaphore_signal(barrier, inc=1, device_id=(me, mates[j]), device_id_type=MESH)
    loads[0].wait()
    ids = [region[k] for k in range(count)]

    def find(j):
        first, last = jnp.int32(-1), jnp.int32(-1)
        for k in range(count):
            here = (ids[k] >> log2(NT)) == peers[j]
            last = jnp.where(here, k, last)
            first = jnp.where(here & (first < 0), k, first)
        entries = [jnp.maximum(first, 0), jnp.maximum(last, 0)]
        for slot, there in enumerate((first >= 0, last != first)):
            tile = jnp.where(there, region[entries[slot]] & (NT - 1), -1)
            tags[j, slot : slot + 1, :] = jnp.full((1, LANES), tile, jnp.int32)
        return entries

    def pack_section(j, entries):
        for slot, entry in enumerate(entries):
            values = tiles[entry].astype(jnp.float32)
            held = 3 * levels
            for k in range(parts):
                spread[j, slot, pl.ds(k, held, stride=parts), :] = values[:, k * LANES : (k + 1) * LANES]
            for c in range(3):
                piece = spread[j, slot, c * rows : (c + 1) * rows, :]
                pack[j, c, slot * rows : (slot + 1) * rows, :] = piece.astype(jnp.bfloat16)

    def send_tags(j):
        copy = pltpu.make_async_remote_copy(
            src_ref=tags.at[j],
            dst_ref=tags_in.at[j],
            send_sem=send0.at[j],
            recv_sem=recv0.at[j],
            device_id=(peers[j], mine),
            device_id_type=MESH,
        )
        copy.start()
        return copy

    def send_section(n, j):
        copy = pltpu.make_async_remote_copy(
            src_ref=pack.at[j, pl.ds(*CHUNKS[n])],
            dst_ref=land.at[j, pl.ds(*CHUNKS[n])],
            send_sem=send1.at[n, j],
            recv_sem=recv1.at[n, j],
            device_id=(peers[j], mine),
            device_id_type=MESH,
        )
        copy.start()
        return copy

    def send_columns(n, j):
        copy = pltpu.make_async_remote_copy(
            src_ref=stage.at[mates[j], pl.ds(*CHUNKS[n])],
            dst_ref=grad.at[mine, pl.ds(*CHUNKS[n])],
            send_sem=send2.at[n, j],
            recv_sem=recv2.at[n, j],
            device_id=(me, mates[j]),
            device_id_type=MESH,
        )
        copy.start()
        return copy

    order = list(range(groups - 1, 0, -1))
    entries = [find(j) for j in range(groups)]
    loads[1].wait()
    sections, columns = {}, {}
    for i, j in enumerate(order):
        pack_section(j, entries[j])
        if i == 0:
            pl.semaphore_wait(barrier, groups + slabs - 2)
        sections[0, j] = send_section(0, j)
    for n in range(1, len(CHUNKS)):
        for j in order:
            sections[n, j] = send_section(n, j)
    numbers = {j: send_tags(j) for j in order}
    pack_section(0, entries[0])
    loads[2].wait()
    weights[...] = spread_smoother(band, depth, slabs, cols, block)

    def reduce(c, t):
        total = jnp.zeros((rows // 8, 8, LANES), jnp.float32)
        for j in range(groups):
            held = pack if j == 0 else land
            number = tags[j] if j == 0 else tags_in[j]
            for slot in range(CAP):
                term = held[j, c, slot * rows : (slot + 1) * rows, :].astype(jnp.float32)
                tag = jnp.broadcast_to(number[slot : slot + 1], (8, LANES))
                total += jnp.where((tag == t)[None], term.reshape(rows // 8, 8, LANES), 0.0)
        total = total.reshape(levels, parts, LANES)
        for q in range(per_tile):
            piece = total[:, q * cols : (q + 1) * cols, :].reshape(levels * cols, LANES)
            if block > levels * cols:
                fill = jnp.zeros((block - levels * cols, LANES), jnp.float32)
                piece = jnp.concatenate([piece, fill], axis=0)
            stage[t * per_tile + q, c] = piece.astype(jnp.bfloat16)

    for n, (low, size) in enumerate(CHUNKS):
        for j in order:
            if n == 0:
                numbers[j].wait_recv()
            sections[n, j].wait_recv()
        for other in range(NT - 1, -1, -1):
            t = (mine >> log2(per_tile)) ^ other
            for c in range(low, low + size):
                reduce(c, t)
            for j in range(max(other * per_tile, 1), (other + 1) * per_tile):
                columns[n, j] = send_columns(n, j)
        grad[mine, pl.ds(low, size)] = stage[mine, pl.ds(low, size)]

    for n, (low, size) in enumerate(CHUNKS):
        for j in range(1, slabs):
            columns[n, j].wait_recv()
        for c in range(low, low + size):
            gathered = grad[:, c].reshape(slabs * block, LANES)
            smooth = jnp.dot(weights[...], gathered, preferred_element_type=jnp.float32)
            for k in range(cols):
                out_ref[c, :, k * LANES : (k + 1) * LANES] = smooth[k * depth : (k + 1) * depth]
    for copy in [*numbers.values(), *sections.values(), *columns.values()]:
        copy.wait_send()


def shards(kernel_tiles, region, band_width):
    tiles, ids = kernel_tiles[0, 0], region[0, 0]
    groups, slabs = lax.axis_size("ev"), lax.axis_size("blk")
    count, held, width = tiles.shape
    levels = held // 3
    depth = levels * slabs
    parts = width // LANES
    cols = NT * parts // slabs
    block = -(-levels * cols // 16) * 16
    dims = (groups, slabs, count, levels, parts, cols, block)
    rows = levels * parts
    message = CAP * rows
    return pl.pallas_call(
        functools.partial(kernel, dims),
        out_shape=pltpu.VMEM((3, depth, cols * LANES), jnp.float32),
        in_specs=[pl.BlockSpec(memory_space=pltpu.HBM)] * 3,
        out_specs=pl.BlockSpec(memory_space=pltpu.VMEM),
        scratch_shapes=[
            pltpu.VMEM(tiles.shape, jnp.bfloat16),
            pltpu.SMEM(ids.shape, jnp.int32),
            pltpu.SMEM(band_width.shape, jnp.int32),
            pltpu.VMEM((groups, CAP, held * parts, LANES), jnp.float32),
            pltpu.VMEM((groups, CAP, LANES), jnp.int32),
            pltpu.VMEM((groups, CAP, LANES), jnp.int32),
            pltpu.VMEM((groups, 3, message, LANES), jnp.bfloat16),
            pltpu.VMEM((groups, 3, message, LANES), jnp.bfloat16),
            pltpu.VMEM((slabs, 3, block, LANES), jnp.bfloat16),
            pltpu.VMEM((slabs, 3, block, LANES), jnp.bfloat16),
            pltpu.VMEM((cols * depth, slabs * block), jnp.bfloat16),
            pltpu.SemaphoreType.DMA((3,)),
            pltpu.SemaphoreType.DMA((groups,)),
            pltpu.SemaphoreType.DMA((groups,)),
            pltpu.SemaphoreType.DMA((len(CHUNKS), groups)),
            pltpu.SemaphoreType.DMA((len(CHUNKS), groups)),
            pltpu.SemaphoreType.DMA((len(CHUNKS), slabs)),
            pltpu.SemaphoreType.DMA((len(CHUNKS), slabs)),
        ],
        compiler_params=pltpu.CompilerParams(
            collective_id=0, has_side_effects=True, vmem_limit_bytes=48 * 1024 * 1024
        ),
    )(*[pltpu.with_memory_space_constraint(a, pltpu.HBM) for a in (tiles, ids, band_width)])


def solution(mesh):
    in_specs = (P("ev", "blk", None, None, None), P("ev", "blk", None), P())
    out_specs = P(None, None, ("ev", "blk"))
    return jax.shard_map(shards, mesh=mesh, in_specs=in_specs, out_specs=out_specs, check_vma=False)
```

```python
import functools

import jax
import jax.numpy as jnp
from jax import lax
from jax.experimental import pallas as pl
from jax.experimental.pallas import tpu as pltpu
from jax.sharding import PartitionSpec as P

NT = 4
CAP = 2
LAYERS = 8
LANES = 128
CHUNKS = ((0, 2), (2, 1))
MESH = pl.DeviceIdType.MESH


def log2(n):
    assert n & (n - 1) == 0
    return n.bit_length() - 1


def spread_smoother(band, depth, slabs, cols, block):
    shape = (cols * depth, slabs * block)
    row = lax.broadcasted_iota(jnp.int32, shape, 0)
    col = lax.broadcasted_iota(jnp.int32, shape, 1)
    level = row & (depth - 1)
    within = col & (block - 1)
    levels = depth // slabs
    source = (col >> log2(block)) * levels + (within >> log2(cols))
    layer = level >> log2(depth // LAYERS)
    half = jnp.zeros(shape, jnp.int32)
    for n in range(LAYERS):
        half = jnp.where(layer == n, band[n], half)
    weight = jnp.maximum(half + 1 - jnp.abs(level - source), 0)
    weight = jnp.where(within < levels * cols, weight, 0).astype(jnp.float32)
    total = jnp.sum(weight, axis=1, keepdims=True) * (1.0 / cols)
    same = (row >> log2(depth)) == (within & (cols - 1))
    return jnp.where(same, weight / total, 0.0).astype(jnp.bfloat16)


def kernel(dims, tiles_hbm, region_hbm, band_hbm, out_ref, tiles, region, band, spread, tags, tags_in, pack, land,
           stage, grad, weights, in_sem, send0, recv0, send1, recv1, send2, recv2):
    groups, slabs, count, levels, parts, cols, block = dims
    assert groups & (groups - 1) == 0 and slabs & (slabs - 1) == 0
    depth = levels * slabs
    per_tile = slabs // NT
    rows = levels * parts
    me, mine = lax.axis_index("ev"), lax.axis_index("blk")
    peers = [me ^ j for j in range(groups)]
    mates = [mine ^ j for j in range(slabs)]

    loads = [
        pltpu.make_async_copy(region_hbm, region, in_sem.at[0]),
        pltpu.make_async_copy(tiles_hbm, tiles, in_sem.at[1]),
        pltpu.make_async_copy(band_hbm, band, in_sem.at[2]),
    ]
    for load in loads:
        load.start()
    barrier = pltpu.get_barrier_semaphore()
    for j in range(1, groups):
        pl.semaphore_signal(barrier, inc=1, device_id=(peers[j], mine), device_id_type=MESH)
    for j in range(1, slabs):
        pl.semaphore_signal(barrier, inc=1, device_id=(me, mates[j]), device_id_type=MESH)
    loads[0].wait()
    ids = [region[k] for k in range(count)]

    def find(j):
        first, last = jnp.int32(-1), jnp.int32(-1)
        for k in range(count):
            here = (ids[k] >> log2(NT)) == peers[j]
            last = jnp.where(here, k, last)
            first = jnp.where(here & (first < 0), k, first)
        entries = [jnp.maximum(first, 0), jnp.maximum(last, 0)]
        for slot, there in enumerate((first >= 0, last != first)):
            tile = jnp.where(there, region[entries[slot]] & (NT - 1), -1)
            tags[j, slot : slot + 1, :] = jnp.full((1, LANES), tile, jnp.int32)
        return entries

    def pack_section(j, entries):
        for slot, entry in enumerate(entries):
            values = tiles[entry].astype(jnp.float32)
            held = 3 * levels
            for k in range(parts):
                spread[j, slot, pl.ds(k, held, stride=parts), :] = values[:, k * LANES : (k + 1) * LANES]
            for c in range(3):
                piece = spread[j, slot, c * rows : (c + 1) * rows, :]
                pack[j, c, slot * rows : (slot + 1) * rows, :] = piece.astype(jnp.bfloat16)

    def send_tags(j):
        copy = pltpu.make_async_remote_copy(
            src_ref=tags.at[j],
            dst_ref=tags_in.at[j],
            send_sem=send0.at[j],
            recv_sem=recv0.at[j],
            device_id=(peers[j], mine),
            device_id_type=MESH,
        )
        copy.start()
        return copy

    def send_section(n, j):
        copy = pltpu.make_async_remote_copy(
            src_ref=pack.at[j, pl.ds(*CHUNKS[n])],
            dst_ref=land.at[j, pl.ds(*CHUNKS[n])],
            send_sem=send1.at[n, j],
            recv_sem=recv1.at[n, j],
            device_id=(peers[j], mine),
            device_id_type=MESH,
        )
        copy.start()
        return copy

    def send_columns(n, j):
        copy = pltpu.make_async_remote_copy(
            src_ref=stage.at[mates[j], pl.ds(*CHUNKS[n])],
            dst_ref=grad.at[mine, pl.ds(*CHUNKS[n])],
            send_sem=send2.at[n, j],
            recv_sem=recv2.at[n, j],
            device_id=(me, mates[j]),
            device_id_type=MESH,
        )
        copy.start()
        return copy

    order = list(range(groups - 1, 0, -1))
    entries = [find(j) for j in range(groups)]
    loads[1].wait()
    sections, columns = {}, {}
    for i, j in enumerate(order):
        pack_section(j, entries[j])
        if i == 0:
            pl.semaphore_wait(barrier, groups + slabs - 2)
        sections[0, j] = send_section(0, j)
    for n in range(1, len(CHUNKS)):
        for j in order:
            sections[n, j] = send_section(n, j)
    numbers = {j: send_tags(j) for j in order}
    pack_section(0, entries[0])
    loads[2].wait()
    weights[...] = spread_smoother(band, depth, slabs, cols, block)

    def reduce(c, t):
        total = jnp.zeros((rows // 8, 8, LANES), jnp.float32)
        for j in range(groups):
            held = pack if j == 0 else land
            number = tags[j] if j == 0 else tags_in[j]
            for slot in range(CAP):
                term = held[j, c, slot * rows : (slot + 1) * rows, :].astype(jnp.float32)
                tag = jnp.broadcast_to(number[slot : slot + 1], (8, LANES))
                total += jnp.where((tag == t)[None], term.reshape(rows // 8, 8, LANES), 0.0)
        total = total.reshape(levels, parts, LANES)
        for q in range(per_tile):
            piece = total[:, q * cols : (q + 1) * cols, :].reshape(levels * cols, LANES)
            if block > levels * cols:
                fill = jnp.zeros((block - levels * cols, LANES), jnp.float32)
                piece = jnp.concatenate([piece, fill], axis=0)
            stage[t * per_tile + q, c] = piece.astype(jnp.bfloat16)

    for n, (low, size) in enumerate(CHUNKS):
        for j in order:
            if n == 0:
                numbers[j].wait_recv()
            sections[n, j].wait_recv()
        for other in range(NT - 1, -1, -1):
            t = (mine >> log2(per_tile)) ^ other
            for c in range(low, low + size):
                reduce(c, t)
            for j in range(max(other * per_tile, 1), (other + 1) * per_tile):
                columns[n, j] = send_columns(n, j)
        grad[mine, pl.ds(low, size)] = stage[mine, pl.ds(low, size)]

    for n, (low, size) in enumerate(CHUNKS):
        for j in range(1, slabs):
            columns[n, j].wait_recv()
        for c in range(low, low + size):
            gathered = grad[:, c].reshape(slabs * block, LANES)
            smooth = jnp.dot(weights[...], gathered, preferred_element_type=jnp.float32)
            for k in range(cols):
                out_ref[c, :, k * LANES : (k + 1) * LANES] = smooth[k * depth : (k + 1) * depth]
    for copy in [*numbers.values(), *sections.values(), *columns.values()]:
        copy.wait_send()


def shards(kernel_tiles, region, band_width):
    tiles, ids = kernel_tiles[0, 0], region[0, 0]
    groups, slabs = lax.axis_size("ev"), lax.axis_size("blk")
    count, held, width = tiles.shape
    levels = held // 3
    depth = levels * slabs
    parts = width // LANES
    cols = NT * parts // slabs
    block = -(-levels * cols // 16) * 16
    dims = (groups, slabs, count, levels, parts, cols, block)
    rows = levels * parts
    message = CAP * rows
    return pl.pallas_call(
        functools.partial(kernel, dims),
        out_shape=pltpu.VMEM((3, depth, cols * LANES), jnp.float32),
        in_specs=[pl.BlockSpec(memory_space=pltpu.HBM)] * 3,
        out_specs=pl.BlockSpec(memory_space=pltpu.VMEM),
        scratch_shapes=[
            pltpu.VMEM(tiles.shape, jnp.bfloat16),
            pltpu.SMEM(ids.shape, jnp.int32),
            pltpu.SMEM(band_width.shape, jnp.int32),
            pltpu.VMEM((groups, CAP, held * parts, LANES), jnp.float32),
            pltpu.VMEM((groups, CAP, LANES), jnp.int32),
            pltpu.VMEM((groups, CAP, LANES), jnp.int32),
            pltpu.VMEM((groups, 3, message, LANES), jnp.bfloat16),
            pltpu.VMEM((groups, 3, message, LANES), jnp.bfloat16),
            pltpu.VMEM((slabs, 3, block, LANES), jnp.bfloat16),
            pltpu.VMEM((slabs, 3, block, LANES), jnp.bfloat16),
            pltpu.VMEM((cols * depth, slabs * block), jnp.bfloat16),
            pltpu.SemaphoreType.DMA((3,)),
            pltpu.SemaphoreType.DMA((groups,)),
            pltpu.SemaphoreType.DMA((groups,)),
            pltpu.SemaphoreType.DMA((len(CHUNKS), groups)),
            pltpu.SemaphoreType.DMA((len(CHUNKS), groups)),
            pltpu.SemaphoreType.DMA((len(CHUNKS), slabs)),
            pltpu.SemaphoreType.DMA((len(CHUNKS), slabs)),
        ],
        compiler_params=pltpu.CompilerParams(
            collective_id=0, has_side_effects=True, vmem_limit_bytes=48 * 1024 * 1024
        ),
    )(*[pltpu.with_memory_space_constraint(a, pltpu.HBM) for a in (tiles, ids, band_width)])


def solution(mesh):
    in_specs = (P("ev", "blk", None, None, None), P("ev", "blk", None), P())
    out_specs = P(None, None, ("ev", "blk"))
    return jax.shard_map(shards, mesh=mesh, in_specs=in_specs, out_specs=out_specs, check_vma=False)
```

```python
import functools

import jax
import jax.numpy as jnp
from jax import lax
from jax.experimental import pallas as pl
from jax.experimental.pallas import tpu as pltpu
from jax.sharding import PartitionSpec as P

NT = 4
CAP = 2
LAYERS = 8
LANES = 128
LOADS = 3
CHUNKS = ((0, 3),)
MESH = pl.DeviceIdType.MESH


def log2(n):
    assert n & (n - 1) == 0
    return n.bit_length() - 1


def spread_smoother(band, depth, slabs, cols, block):
    shape = (cols * depth, slabs * block)
    row = lax.broadcasted_iota(jnp.int32, shape, 0)
    col = lax.broadcasted_iota(jnp.int32, shape, 1)
    level = row & (depth - 1)
    within = col & (block - 1)
    levels = depth // slabs
    source = (col >> log2(block)) * levels + (within >> log2(cols))
    layer = level >> log2(depth // LAYERS)
    half = jnp.zeros(shape, jnp.int32)
    for n in range(LAYERS):
        half = jnp.where(layer == n, band[n], half)
    weight = jnp.maximum(half + 1 - jnp.abs(level - source), 0)
    weight = jnp.where(within < levels * cols, weight, 0).astype(jnp.float32)
    total = jnp.sum(weight, axis=1, keepdims=True) * (1.0 / cols)
    same = (row >> log2(depth)) == (within & (cols - 1))
    return jnp.where(same, weight / total, 0.0).astype(jnp.bfloat16)


def kernel(dims, tiles_hbm, region_hbm, band_hbm, out_ref, tiles, region, band, spread, tags, tags_in, pack, land,
           partial, stage, grad, weights, in_sem, send0, recv0, send1, recv1, send2, recv2):
    groups, slabs, count, levels, parts, cols, block = dims
    assert groups & (groups - 1) == 0 and slabs & (slabs - 1) == 0
    depth = levels * slabs
    per_tile = slabs // NT
    rows = levels * parts
    me, mine = lax.axis_index("ev"), lax.axis_index("blk")
    peers = [me ^ j for j in range(groups)]
    mates = [mine ^ j for j in range(slabs)]

    loads = [
        pltpu.make_async_copy(region_hbm, region, in_sem.at[0]),
        pltpu.make_async_copy(band_hbm, band, in_sem.at[1]),
    ]
    share = -(-count // LOADS)
    for n, low in enumerate(range(0, count, share)):
        part = pl.ds(low, min(share, count - low))
        loads.append(pltpu.make_async_copy(tiles_hbm.at[part], tiles.at[part], in_sem.at[2 + n]))
    for load in loads:
        load.start()
    barrier = pltpu.get_barrier_semaphore()
    for j in range(1, groups):
        pl.semaphore_signal(barrier, inc=1, device_id=(peers[j], mine), device_id_type=MESH)
    for j in range(1, slabs):
        pl.semaphore_signal(barrier, inc=1, device_id=(me, mates[j]), device_id_type=MESH)
    loads[0].wait()
    ids = [region[k] for k in range(count)]

    def find(j):
        first, last = jnp.int32(-1), jnp.int32(-1)
        for k in range(count):
            here = (ids[k] >> log2(NT)) == peers[j]
            last = jnp.where(here, k, last)
            first = jnp.where(here & (first < 0), k, first)
        entries = [jnp.maximum(first, 0), jnp.maximum(last, 0)]
        for slot, there in enumerate((first >= 0, last != first)):
            tile = jnp.where(there, region[entries[slot]] & (NT - 1), -1)
            tags[j, slot : slot + 1, :] = jnp.full((1, LANES), tile, jnp.int32)
        return entries

    def pack_section(j, entries):
        for slot, entry in enumerate(entries):
            values = tiles[entry].astype(jnp.float32)
            held = 3 * levels
            for k in range(parts):
                spread[j, slot, pl.ds(k, held, stride=parts), :] = values[:, k * LANES : (k + 1) * LANES]
            for c in range(3):
                piece = spread[j, slot, c * rows : (c + 1) * rows, :]
                pack[j, c, slot * rows : (slot + 1) * rows, :] = piece.astype(jnp.bfloat16)

    def send_tags(j):
        copy = pltpu.make_async_remote_copy(
            src_ref=tags.at[j],
            dst_ref=tags_in.at[j],
            send_sem=send0.at[j],
            recv_sem=recv0.at[j],
            device_id=(peers[j], mine),
            device_id_type=MESH,
        )
        copy.start()
        return copy

    def send_section(n, j):
        copy = pltpu.make_async_remote_copy(
            src_ref=pack.at[j, pl.ds(*CHUNKS[n])],
            dst_ref=land.at[j, pl.ds(*CHUNKS[n])],
            send_sem=send1.at[n, j],
            recv_sem=recv1.at[n, j],
            device_id=(peers[j], mine),
            device_id_type=MESH,
        )
        copy.start()
        return copy

    def send_columns(n, j):
        copy = pltpu.make_async_remote_copy(
            src_ref=stage.at[mates[j], pl.ds(*CHUNKS[n])],
            dst_ref=grad.at[mine, pl.ds(*CHUNKS[n])],
            send_sem=send2.at[n, j],
            recv_sem=recv2.at[n, j],
            device_id=(me, mates[j]),
            device_id_type=MESH,
        )
        copy.start()
        return copy

    order = list(range(groups - 1, 0, -1))
    near, far = list(range(groups // 2)), list(range(groups // 2, groups))
    entries = [find(j) for j in range(groups)]
    for load in loads[2:]:
        load.wait()
    sections, columns = {}, {}
    for i, j in enumerate(order):
        pack_section(j, entries[j])
        if i == 0:
            pl.semaphore_wait(barrier, groups + slabs - 2)
        sections[0, j] = send_section(0, j)
    for n in range(1, len(CHUNKS)):
        for j in order:
            sections[n, j] = send_section(n, j)
    numbers = {j: send_tags(j) for j in order}
    pack_section(0, entries[0])
    loads[1].wait()
    weights[...] = spread_smoother(band, depth, slabs, cols, block)

    def add_terms(total, c, t, sources):
        for j in sources:
            held = pack if j == 0 else land
            number = tags[j] if j == 0 else tags_in[j]
            for slot in range(CAP):
                term = held[j, c, slot * rows : (slot + 1) * rows, :].astype(jnp.float32)
                tag = jnp.broadcast_to(number[slot : slot + 1], (8, LANES))
                total += jnp.where((tag == t)[None], term.reshape(rows // 8, 8, LANES), 0.0)
        return total

    def reduce(c, t):
        total = add_terms(partial[t, c].reshape(rows // 8, 8, LANES), c, t, far)
        total = total.reshape(levels, parts, LANES)
        for q in range(per_tile):
            piece = total[:, q * cols : (q + 1) * cols, :].reshape(levels * cols, LANES)
            if block > levels * cols:
                fill = jnp.zeros((block - levels * cols, LANES), jnp.float32)
                piece = jnp.concatenate([piece, fill], axis=0)
            stage[t * per_tile + q, c] = piece.astype(jnp.bfloat16)

    for n, (low, size) in enumerate(CHUNKS):
        for j in near[1:]:
            if n == 0:
                numbers[j].wait_recv()
            sections[n, j].wait_recv()
        for c in range(low, low + size):
            for t in range(NT):
                zero = jnp.zeros((rows // 8, 8, LANES), jnp.float32)
                partial[t, c] = add_terms(zero, c, t, near).reshape(rows, LANES)
        for j in far:
            if n == 0:
                numbers[j].wait_recv()
            sections[n, j].wait_recv()
        for other in range(NT - 1, -1, -1):
            t = (mine >> log2(per_tile)) ^ other
            for c in range(low, low + size):
                reduce(c, t)
            for j in range(max(other * per_tile, 1), (other + 1) * per_tile):
                columns[n, j] = send_columns(n, j)
        grad[mine, pl.ds(low, size)] = stage[mine, pl.ds(low, size)]

    for n, (low, size) in enumerate(CHUNKS):
        for j in range(1, slabs):
            columns[n, j].wait_recv()
        for c in range(low, low + size):
            gathered = grad[:, c].reshape(slabs * block, LANES)
            smooth = jnp.dot(weights[...], gathered, preferred_element_type=jnp.float32)
            for k in range(cols):
                out_ref[c, :, k * LANES : (k + 1) * LANES] = smooth[k * depth : (k + 1) * depth]
    for copy in [*numbers.values(), *sections.values(), *columns.values()]:
        copy.wait_send()


def shards(kernel_tiles, region, band_width):
    tiles, ids = kernel_tiles[0, 0], region[0, 0]
    groups, slabs = lax.axis_size("ev"), lax.axis_size("blk")
    count, held, width = tiles.shape
    levels = held // 3
    depth = levels * slabs
    parts = width // LANES
    cols = NT * parts // slabs
    block = -(-levels * cols // 16) * 16
    dims = (groups, slabs, count, levels, parts, cols, block)
    rows = levels * parts
    message = CAP * rows
    return pl.pallas_call(
        functools.partial(kernel, dims),
        out_shape=pltpu.VMEM((3, depth, cols * LANES), jnp.float32),
        in_specs=[pl.BlockSpec(memory_space=pltpu.HBM)] * 3,
        out_specs=pl.BlockSpec(memory_space=pltpu.VMEM),
        scratch_shapes=[
            pltpu.VMEM(tiles.shape, jnp.bfloat16),
            pltpu.SMEM(ids.shape, jnp.int32),
            pltpu.SMEM(band_width.shape, jnp.int32),
            pltpu.VMEM((groups, CAP, held * parts, LANES), jnp.float32),
            pltpu.VMEM((groups, CAP, LANES), jnp.int32),
            pltpu.VMEM((groups, CAP, LANES), jnp.int32),
            pltpu.VMEM((groups, 3, message, LANES), jnp.bfloat16),
            pltpu.VMEM((groups, 3, message, LANES), jnp.bfloat16),
            pltpu.VMEM((NT, 3, rows, LANES), jnp.float32),
            pltpu.VMEM((slabs, 3, block, LANES), jnp.bfloat16),
            pltpu.VMEM((slabs, 3, block, LANES), jnp.bfloat16),
            pltpu.VMEM((cols * depth, slabs * block), jnp.bfloat16),
            pltpu.SemaphoreType.DMA((2 + LOADS,)),
            pltpu.SemaphoreType.DMA((groups,)),
            pltpu.SemaphoreType.DMA((groups,)),
            pltpu.SemaphoreType.DMA((len(CHUNKS), groups)),
            pltpu.SemaphoreType.DMA((len(CHUNKS), groups)),
            pltpu.SemaphoreType.DMA((len(CHUNKS), slabs)),
            pltpu.SemaphoreType.DMA((len(CHUNKS), slabs)),
        ],
        compiler_params=pltpu.CompilerParams(
            collective_id=0, has_side_effects=True, vmem_limit_bytes=48 * 1024 * 1024
        ),
    )(*[pltpu.with_memory_space_constraint(a, pltpu.HBM) for a in (tiles, ids, band_width)])


def solution(mesh):
    in_specs = (P("ev", "blk", None, None, None), P("ev", "blk", None), P())
    out_specs = P(None, None, ("ev", "blk"))
    return jax.shard_map(shards, mesh=mesh, in_specs=in_specs, out_specs=out_specs, check_vma=False)
```

```python
import functools

import jax
import jax.numpy as jnp
from jax import lax
from jax.experimental import pallas as pl
from jax.experimental.pallas import tpu as pltpu
from jax.sharding import PartitionSpec as P

NT = 4
CAP = 2
LAYERS = 8
LANES = 128
LOADS = 3
CHUNKS = ((0, 3),)
MESH = pl.DeviceIdType.MESH


def log2(n):
    assert n & (n - 1) == 0
    return n.bit_length() - 1


def spread_smoother(band, depth, slabs, cols, block):
    shape = (cols * depth, slabs * block)
    row = lax.broadcasted_iota(jnp.int32, shape, 0)
    col = lax.broadcasted_iota(jnp.int32, shape, 1)
    level = row & (depth - 1)
    within = col & (block - 1)
    levels = depth // slabs
    source = (col >> log2(block)) * levels + (within >> log2(cols))
    layer = level >> log2(depth // LAYERS)
    half = jnp.zeros(shape, jnp.int32)
    for n in range(LAYERS):
        half = jnp.where(layer == n, band[n], half)
    weight = jnp.maximum(half + 1 - jnp.abs(level - source), 0)
    weight = jnp.where(within < levels * cols, weight, 0).astype(jnp.float32)
    total = jnp.sum(weight, axis=1, keepdims=True) * (1.0 / cols)
    same = (row >> log2(depth)) == (within & (cols - 1))
    return jnp.where(same, weight / total, 0.0).astype(jnp.bfloat16)


def kernel(dims, tiles_hbm, region_hbm, band_hbm, out_ref, tiles, region, band, spread, tags, tags_in, pack, land,
           partial, stage, grad, weights, in_sem, send0, recv0, send1, recv1, send2, recv2):
    groups, slabs, count, levels, parts, cols, block = dims
    assert groups & (groups - 1) == 0 and slabs & (slabs - 1) == 0
    depth = levels * slabs
    per_tile = slabs // NT
    rows = levels * parts
    me, mine = lax.axis_index("ev"), lax.axis_index("blk")
    peers = [me ^ j for j in range(groups)]
    mates = [mine ^ j for j in range(slabs)]

    loads = [
        pltpu.make_async_copy(region_hbm, region, in_sem.at[0]),
        pltpu.make_async_copy(band_hbm, band, in_sem.at[1]),
    ]
    share = -(-count // LOADS)
    for n, low in enumerate(range(0, count, share)):
        part = pl.ds(low, min(share, count - low))
        loads.append(pltpu.make_async_copy(tiles_hbm.at[part], tiles.at[part], in_sem.at[2 + n]))
    for load in loads:
        load.start()
    barrier = pltpu.get_barrier_semaphore()
    for j in range(1, groups):
        pl.semaphore_signal(barrier, inc=1, device_id=(peers[j], mine), device_id_type=MESH)
    for j in range(1, slabs):
        pl.semaphore_signal(barrier, inc=1, device_id=(me, mates[j]), device_id_type=MESH)
    loads[0].wait()
    ids = [region[k] for k in range(count)]

    def find(j):
        first, last = jnp.int32(-1), jnp.int32(-1)
        for k in range(count):
            here = (ids[k] >> log2(NT)) == peers[j]
            last = jnp.where(here, k, last)
            first = jnp.where(here & (first < 0), k, first)
        entries = [jnp.maximum(first, 0), jnp.maximum(last, 0)]
        for slot, there in enumerate((first >= 0, last != first)):
            tile = jnp.where(there, region[entries[slot]] & (NT - 1), -1)
            tags[j, slot : slot + 1, :] = jnp.full((1, LANES), tile, jnp.int32)
        return entries

    def pack_section(j, entries):
        for slot, entry in enumerate(entries):
            values = tiles[entry].astype(jnp.float32)
            held = 3 * levels
            for k in range(parts):
                spread[j, slot, pl.ds(k, held, stride=parts), :] = values[:, k * LANES : (k + 1) * LANES]
            for c in range(3):
                piece = spread[j, slot, c * rows : (c + 1) * rows, :]
                pack[j, c, slot * rows : (slot + 1) * rows, :] = piece.astype(jnp.bfloat16)

    def send_tags(j):
        copy = pltpu.make_async_remote_copy(
            src_ref=tags.at[j],
            dst_ref=tags_in.at[j],
            send_sem=send0.at[j],
            recv_sem=recv0.at[j],
            device_id=(peers[j], mine),
            device_id_type=MESH,
        )
        copy.start()
        return copy

    def send_section(n, j):
        copy = pltpu.make_async_remote_copy(
            src_ref=pack.at[j, n],
            dst_ref=land.at[j, n],
            send_sem=send1.at[n, j],
            recv_sem=recv1.at[n, j],
            device_id=(peers[j], mine),
            device_id_type=MESH,
        )
        copy.start()
        return copy

    def send_columns(n, j):
        copy = pltpu.make_async_remote_copy(
            src_ref=stage.at[mates[j], pl.ds(*CHUNKS[n])],
            dst_ref=grad.at[mine, pl.ds(*CHUNKS[n])],
            send_sem=send2.at[n, j],
            recv_sem=recv2.at[n, j],
            device_id=(me, mates[j]),
            device_id_type=MESH,
        )
        copy.start()
        return copy

    order = list(range(groups - 1, 0, -1))
    near, far = list(range(groups // 2)), list(range(groups // 2, groups))
    entries = [find(j) for j in range(groups)]
    for load in loads[2:]:
        load.wait()
    sections, columns = {}, {}
    for i, j in enumerate(order):
        pack_section(j, entries[j])
        if i == 0:
            pl.semaphore_wait(barrier, groups + slabs - 2)
        for c in range(3):
            sections[c, j] = send_section(c, j)
    numbers = {j: send_tags(j) for j in order}
    pack_section(0, entries[0])
    loads[1].wait()
    weights[...] = spread_smoother(band, depth, slabs, cols, block)

    def add_terms(total, c, t, sources):
        for j in sources:
            held = pack if j == 0 else land
            number = tags[j] if j == 0 else tags_in[j]
            for slot in range(CAP):
                term = held[j, c, slot * rows : (slot + 1) * rows, :].astype(jnp.float32)
                tag = jnp.broadcast_to(number[slot : slot + 1], (8, LANES))
                total += jnp.where((tag == t)[None], term.reshape(rows // 8, 8, LANES), 0.0)
        return total

    def reduce(c, t):
        total = add_terms(partial[t, c].reshape(rows // 8, 8, LANES), c, t, far)
        total = total.reshape(levels, parts, LANES)
        for q in range(per_tile):
            piece = total[:, q * cols : (q + 1) * cols, :].reshape(levels * cols, LANES)
            if block > levels * cols:
                fill = jnp.zeros((block - levels * cols, LANES), jnp.float32)
                piece = jnp.concatenate([piece, fill], axis=0)
            stage[t * per_tile + q, c] = piece.astype(jnp.bfloat16)

    for n, (low, size) in enumerate(CHUNKS):
        for j in near[1:]:
            if n == 0:
                numbers[j].wait_recv()
            for c in range(low, low + size):
                sections[c, j].wait_recv()
        for c in range(low, low + size):
            for t in range(NT):
                zero = jnp.zeros((rows // 8, 8, LANES), jnp.float32)
                partial[t, c] = add_terms(zero, c, t, near).reshape(rows, LANES)
        for j in far:
            if n == 0:
                numbers[j].wait_recv()
            for c in range(low, low + size):
                sections[c, j].wait_recv()
        for other in range(NT - 1, -1, -1):
            t = (mine >> log2(per_tile)) ^ other
            for c in range(low, low + size):
                reduce(c, t)
            for j in range(max(other * per_tile, 1), (other + 1) * per_tile):
                columns[n, j] = send_columns(n, j)
        grad[mine, pl.ds(low, size)] = stage[mine, pl.ds(low, size)]

    for n, (low, size) in enumerate(CHUNKS):
        for j in range(1, slabs):
            columns[n, j].wait_recv()
        for c in range(low, low + size):
            gathered = grad[:, c].reshape(slabs * block, LANES)
            smooth = jnp.dot(weights[...], gathered, preferred_element_type=jnp.float32)
            for k in range(cols):
                out_ref[c, :, k * LANES : (k + 1) * LANES] = smooth[k * depth : (k + 1) * depth]
    for copy in [*numbers.values(), *sections.values(), *columns.values()]:
        copy.wait_send()


def shards(kernel_tiles, region, band_width):
    tiles, ids = kernel_tiles[0, 0], region[0, 0]
    groups, slabs = lax.axis_size("ev"), lax.axis_size("blk")
    count, held, width = tiles.shape
    levels = held // 3
    depth = levels * slabs
    parts = width // LANES
    cols = NT * parts // slabs
    block = -(-levels * cols // 16) * 16
    dims = (groups, slabs, count, levels, parts, cols, block)
    rows = levels * parts
    message = CAP * rows
    return pl.pallas_call(
        functools.partial(kernel, dims),
        out_shape=pltpu.VMEM((3, depth, cols * LANES), jnp.float32),
        in_specs=[pl.BlockSpec(memory_space=pltpu.HBM)] * 3,
        out_specs=pl.BlockSpec(memory_space=pltpu.VMEM),
        scratch_shapes=[
            pltpu.VMEM(tiles.shape, jnp.bfloat16),
            pltpu.SMEM(ids.shape, jnp.int32),
            pltpu.SMEM(band_width.shape, jnp.int32),
            pltpu.VMEM((groups, CAP, held * parts, LANES), jnp.float32),
            pltpu.VMEM((groups, CAP, LANES), jnp.int32),
            pltpu.VMEM((groups, CAP, LANES), jnp.int32),
            pltpu.VMEM((groups, 3, message, LANES), jnp.bfloat16),
            pltpu.VMEM((groups, 3, message, LANES), jnp.bfloat16),
            pltpu.VMEM((NT, 3, rows, LANES), jnp.float32),
            pltpu.VMEM((slabs, 3, block, LANES), jnp.bfloat16),
            pltpu.VMEM((slabs, 3, block, LANES), jnp.bfloat16),
            pltpu.VMEM((cols * depth, slabs * block), jnp.bfloat16),
            pltpu.SemaphoreType.DMA((2 + LOADS,)),
            pltpu.SemaphoreType.DMA((groups,)),
            pltpu.SemaphoreType.DMA((groups,)),
            pltpu.SemaphoreType.DMA((3, groups)),
            pltpu.SemaphoreType.DMA((3, groups)),
            pltpu.SemaphoreType.DMA((len(CHUNKS), slabs)),
            pltpu.SemaphoreType.DMA((len(CHUNKS), slabs)),
        ],
        compiler_params=pltpu.CompilerParams(
            collective_id=0, has_side_effects=True, vmem_limit_bytes=48 * 1024 * 1024
        ),
    )(*[pltpu.with_memory_space_constraint(a, pltpu.HBM) for a in (tiles, ids, band_width)])


def solution(mesh):
    in_specs = (P("ev", "blk", None, None, None), P("ev", "blk", None), P())
    out_specs = P(None, None, ("ev", "blk"))
    return jax.shard_map(shards, mesh=mesh, in_specs=in_specs, out_specs=out_specs, check_vma=False)
```

```python
import functools

import jax
import jax.numpy as jnp
from jax import lax
from jax.experimental import pallas as pl
from jax.experimental.pallas import tpu as pltpu
from jax.sharding import PartitionSpec as P

NT = 4
CAP = 2
LAYERS = 8
LANES = 128
LOADS = 3
CHUNKS = ((0, 3),)
MESH = pl.DeviceIdType.MESH


def log2(n):
    assert n & (n - 1) == 0
    return n.bit_length() - 1


def spread_smoother(band, depth, slabs, cols, block):
    shape = (cols * depth, slabs * block)
    row = lax.broadcasted_iota(jnp.int32, shape, 0)
    col = lax.broadcasted_iota(jnp.int32, shape, 1)
    level = row & (depth - 1)
    within = col & (block - 1)
    levels = depth // slabs
    source = (col >> log2(block)) * levels + (within >> log2(cols))
    layer = level >> log2(depth // LAYERS)
    half = jnp.zeros(shape, jnp.int32)
    for n in range(LAYERS):
        half = jnp.where(layer == n, band[n], half)
    weight = jnp.maximum(half + 1 - jnp.abs(level - source), 0)
    weight = jnp.where(within < levels * cols, weight, 0).astype(jnp.float32)
    total = jnp.sum(weight, axis=1, keepdims=True) * (1.0 / cols)
    same = (row >> log2(depth)) == (within & (cols - 1))
    return jnp.where(same, weight / total, 0.0).astype(jnp.bfloat16)


def kernel(dims, tiles_hbm, region_hbm, band_hbm, out_ref, tiles, region, band, spread, tags, tags_in, pack, land,
           partial, stage, grad, weights, in_sem, send0, recv0, send1, recv1, send2, recv2):
    groups, slabs, count, levels, parts, cols, block = dims
    assert groups & (groups - 1) == 0 and slabs & (slabs - 1) == 0
    depth = levels * slabs
    per_tile = slabs // NT
    rows = levels * parts
    me, mine = lax.axis_index("ev"), lax.axis_index("blk")
    peers = [me ^ j for j in range(groups)]
    mates = [mine ^ j for j in range(slabs)]

    loads = [
        pltpu.make_async_copy(region_hbm, region, in_sem.at[0]),
        pltpu.make_async_copy(band_hbm, band, in_sem.at[1]),
    ]
    share = -(-count // LOADS)
    for n, low in enumerate(range(0, count, share)):
        part = pl.ds(low, min(share, count - low))
        loads.append(pltpu.make_async_copy(tiles_hbm.at[part], tiles.at[part], in_sem.at[2 + n]))
    barrier = pltpu.get_barrier_semaphore()
    for j in range(1, groups):
        pl.semaphore_signal(barrier, inc=1, device_id=(peers[j], mine), device_id_type=MESH)
    for j in range(1, slabs):
        pl.semaphore_signal(barrier, inc=1, device_id=(me, mates[j]), device_id_type=MESH)
    for load in loads:
        load.start()
    loads[0].wait()
    ids = [region[k] for k in range(count)]

    def find(j):
        first, last = jnp.int32(-1), jnp.int32(-1)
        for k in range(count):
            here = (ids[k] >> log2(NT)) == peers[j]
            last = jnp.where(here, k, last)
            first = jnp.where(here & (first < 0), k, first)
        entries = [jnp.maximum(first, 0), jnp.maximum(last, 0)]
        for slot, there in enumerate((first >= 0, last != first)):
            tile = jnp.where(there, region[entries[slot]] & (NT - 1), -1)
            tags[j, slot : slot + 1, :] = jnp.full((1, LANES), tile, jnp.int32)
        return entries

    def pack_section(j, entries):
        for slot, entry in enumerate(entries):
            values = tiles[entry].astype(jnp.float32)
            held = 3 * levels
            for k in range(parts):
                spread[j, slot, pl.ds(k, held, stride=parts), :] = values[:, k * LANES : (k + 1) * LANES]
            for c in range(3):
                piece = spread[j, slot, c * rows : (c + 1) * rows, :]
                pack[j, c, slot * rows : (slot + 1) * rows, :] = piece.astype(jnp.bfloat16)

    def send_tags(j):
        copy = pltpu.make_async_remote_copy(
            src_ref=tags.at[j],
            dst_ref=tags_in.at[j],
            send_sem=send0.at[j],
            recv_sem=recv0.at[j],
            device_id=(peers[j], mine),
            device_id_type=MESH,
        )
        copy.start()
        return copy

    def send_section(n, j):
        copy = pltpu.make_async_remote_copy(
            src_ref=pack.at[j, pl.ds(*CHUNKS[n])],
            dst_ref=land.at[j, pl.ds(*CHUNKS[n])],
            send_sem=send1.at[n, j],
            recv_sem=recv1.at[n, j],
            device_id=(peers[j], mine),
            device_id_type=MESH,
        )
        copy.start()
        return copy

    def send_columns(n, j):
        copy = pltpu.make_async_remote_copy(
            src_ref=stage.at[mates[j], pl.ds(*CHUNKS[n])],
            dst_ref=grad.at[mine, pl.ds(*CHUNKS[n])],
            send_sem=send2.at[n, j],
            recv_sem=recv2.at[n, j],
            device_id=(me, mates[j]),
            device_id_type=MESH,
        )
        copy.start()
        return copy

    order = list(range(groups - 1, 0, -1))
    near, far = list(range(groups // 2)), list(range(groups // 2, groups))
    entries = [find(j) for j in range(groups)]
    for load in loads[2:]:
        load.wait()
    sections, columns = {}, {}
    for i, j in enumerate(order):
        pack_section(j, entries[j])
        if i == 0:
            pl.semaphore_wait(barrier, groups + slabs - 2)
        sections[0, j] = send_section(0, j)
    for n in range(1, len(CHUNKS)):
        for j in order:
            sections[n, j] = send_section(n, j)
    numbers = {j: send_tags(j) for j in order}
    pack_section(0, entries[0])
    loads[1].wait()
    weights[...] = spread_smoother(band, depth, slabs, cols, block)

    def add_terms(total, c, t, sources):
        for j in sources:
            held = pack if j == 0 else land
            number = tags[j] if j == 0 else tags_in[j]
            for slot in range(CAP):
                term = held[j, c, slot * rows : (slot + 1) * rows, :].astype(jnp.float32)
                tag = jnp.broadcast_to(number[slot : slot + 1], (8, LANES))
                total += jnp.where((tag == t)[None], term.reshape(rows // 8, 8, LANES), 0.0)
        return total

    def reduce(c, t):
        total = add_terms(partial[t, c].reshape(rows // 8, 8, LANES), c, t, far)
        total = total.reshape(levels, parts, LANES)
        for q in range(per_tile):
            piece = total[:, q * cols : (q + 1) * cols, :].reshape(levels * cols, LANES)
            if block > levels * cols:
                fill = jnp.zeros((block - levels * cols, LANES), jnp.float32)
                piece = jnp.concatenate([piece, fill], axis=0)
            stage[t * per_tile + q, c] = piece.astype(jnp.bfloat16)

    for n, (low, size) in enumerate(CHUNKS):
        for j in near[1:]:
            if n == 0:
                numbers[j].wait_recv()
            sections[n, j].wait_recv()
        for c in range(low, low + size):
            for t in range(NT):
                zero = jnp.zeros((rows // 8, 8, LANES), jnp.float32)
                partial[t, c] = add_terms(zero, c, t, near).reshape(rows, LANES)
        for j in far:
            if n == 0:
                numbers[j].wait_recv()
            sections[n, j].wait_recv()
        for other in range(NT - 1, -1, -1):
            t = (mine >> log2(per_tile)) ^ other
            for c in range(low, low + size):
                reduce(c, t)
            for j in range(max(other * per_tile, 1), (other + 1) * per_tile):
                columns[n, j] = send_columns(n, j)
        grad[mine, pl.ds(low, size)] = stage[mine, pl.ds(low, size)]

    for n, (low, size) in enumerate(CHUNKS):
        for j in range(1, slabs):
            columns[n, j].wait_recv()
        for c in range(low, low + size):
            gathered = grad[:, c].reshape(slabs * block, LANES)
            smooth = jnp.dot(weights[...], gathered, preferred_element_type=jnp.float32)
            for k in range(cols):
                out_ref[c, :, k * LANES : (k + 1) * LANES] = smooth[k * depth : (k + 1) * depth]
    for copy in [*numbers.values(), *sections.values(), *columns.values()]:
        copy.wait_send()


def shards(kernel_tiles, region, band_width):
    tiles, ids = kernel_tiles[0, 0], region[0, 0]
    groups, slabs = lax.axis_size("ev"), lax.axis_size("blk")
    count, held, width = tiles.shape
    levels = held // 3
    depth = levels * slabs
    parts = width // LANES
    cols = NT * parts // slabs
    block = -(-levels * cols // 16) * 16
    dims = (groups, slabs, count, levels, parts, cols, block)
    rows = levels * parts
    message = CAP * rows
    return pl.pallas_call(
        functools.partial(kernel, dims),
        out_shape=pltpu.VMEM((3, depth, cols * LANES), jnp.float32),
        in_specs=[pl.BlockSpec(memory_space=pltpu.HBM)] * 3,
        out_specs=pl.BlockSpec(memory_space=pltpu.VMEM),
        scratch_shapes=[
            pltpu.VMEM(tiles.shape, jnp.bfloat16),
            pltpu.SMEM(ids.shape, jnp.int32),
            pltpu.SMEM(band_width.shape, jnp.int32),
            pltpu.VMEM((groups, CAP, held * parts, LANES), jnp.float32),
            pltpu.VMEM((groups, CAP, LANES), jnp.int32),
            pltpu.VMEM((groups, CAP, LANES), jnp.int32),
            pltpu.VMEM((groups, 3, message, LANES), jnp.bfloat16),
            pltpu.VMEM((groups, 3, message, LANES), jnp.bfloat16),
            pltpu.VMEM((NT, 3, rows, LANES), jnp.float32),
            pltpu.VMEM((slabs, 3, block, LANES), jnp.bfloat16),
            pltpu.VMEM((slabs, 3, block, LANES), jnp.bfloat16),
            pltpu.VMEM((cols * depth, slabs * block), jnp.bfloat16),
            pltpu.SemaphoreType.DMA((2 + LOADS,)),
            pltpu.SemaphoreType.DMA((groups,)),
            pltpu.SemaphoreType.DMA((groups,)),
            pltpu.SemaphoreType.DMA((len(CHUNKS), groups)),
            pltpu.SemaphoreType.DMA((len(CHUNKS), groups)),
            pltpu.SemaphoreType.DMA((len(CHUNKS), slabs)),
            pltpu.SemaphoreType.DMA((len(CHUNKS), slabs)),
        ],
        compiler_params=pltpu.CompilerParams(
            collective_id=0, has_side_effects=True, vmem_limit_bytes=48 * 1024 * 1024
        ),
    )(*[pltpu.with_memory_space_constraint(a, pltpu.HBM) for a in (tiles, ids, band_width)])


def solution(mesh):
    in_specs = (P("ev", "blk", None, None, None), P("ev", "blk", None), P())
    out_specs = P(None, None, ("ev", "blk"))
    return jax.shard_map(shards, mesh=mesh, in_specs=in_specs, out_specs=out_specs, check_vma=False)
```
